128 devices in a mesh: row: 8 (over y, core), col: 16 (over x, z).
Axes of the slice: x: 4, y: 4, z: 4, core: 2. Of those that a mesh axis runs over, the one named last changes fastest.
Arguments:
- alias_factors: bfloat16 [16384, 256], P(('row', 'col')), may hold values from -1.5 to 1.5
- entity_factors: bfloat16 [32768, 256], P(('row', 'col')), may hold values from -1.5 to 1.5
- tile_ids: int32 [8, 16, 96, 2], P('row', 'col'), may hold values from 0 to 15, as said below
- tile_score: bfloat16 [8, 16, 96, 128, 128], P('row', 'col'), may hold values from -6 to 6
- tile_weight: bfloat16 [8, 16, 96, 128, 128], P('row', 'col'), may hold values from 0 to 4, as said below
Outputs:
- alias_new: bfloat16 [16384, 256], P(('row', 'col'))
- entity_new: bfloat16 [32768, 256], P(('row', 'col'))
The draws below stay inside these ranges and needn't reach their ends.
Inputs may be any that keep to these rules, and one draw needn't show every extreme that they name: `tile_ids`: column 0 names a local alias block 0 to 15 of the device's row group, column 1 a local entity block 0 to 15 of its column group; the first min(96, 16) tiles name alias blocks 0, 1, 2 and on in order, the first min(96, 16) tiles name entity blocks likewise; pairs may repeat. `tile_weight`: about half of the entries are observed and positive, the rest zero.
All inputs are finite; a program needn't handle non-finite values.
Results may differ from the reference program's by a relative error of at most 0.012.
The reference program's roundings to bfloat16 on the way count: a program that leaves them out, or rounds other values in their place, can miss the bound.
Values may be sent and summed in bfloat16 or wider, within the bound.
A program may use at most 128 MiB of HBM per device.

```python
import jax
import jax.numpy as jnp
from jax import lax

K = 256
BLK = 128
AB_DEV = 1
EB_DEV = 2
TILES = 96
NA = 128
NE = 256
N_ROW = 8
N_COL = 16


def draw_tile_ids(key, part):
    shape = (N_ROW, N_COL, TILES)
    n_alias = AB_DEV * N_COL
    n_entity = EB_DEV * N_ROW
    keys = jax.random.split(jax.random.fold_in(key, 11), 6)
    place = jnp.arange(TILES, dtype=jnp.int32)[None, None, :]
    alias_perm = jax.random.permutation(keys[0], n_alias).astype(jnp.int32)
    entity_perm = jax.random.permutation(keys[1], n_entity).astype(jnp.int32)
    alias_pick = jnp.minimum(jax.random.randint(keys[2], shape, 0, n_alias), jax.random.randint(keys[3], shape, 0, n_alias))
    entity_pick = jnp.minimum(jax.random.randint(keys[4], shape, 0, n_entity), jax.random.randint(keys[5], shape, 0, n_entity))
    alias_ids = jnp.where(place < n_alias, place, alias_perm[alias_pick])
    entity_ids = jnp.where(place < n_entity, place, entity_perm[entity_pick])
    return jnp.stack([alias_ids, entity_ids], axis=-1).astype(jnp.int32)


def draw_tile_weight(key, part):
    shape = (N_ROW, N_COL, TILES, BLK, BLK)
    keys = jax.random.split(jax.random.fold_in(key, 23), 2)
    observed = jax.random.randint(keys[0], shape, 0, 2).astype(jnp.float32)
    level = jnp.exp(jax.random.uniform(keys[1], shape, jnp.float32, jnp.log(0.5), jnp.log(4.0)))
    return (observed * level).astype(jnp.bfloat16)


def steps_of(own_key, dims, pieces, low, largest):
    def one(dim, shards_of):
        heights = jax.random.uniform(jax.random.fold_in(jax.random.fold_in(own_key, 6), dim), (shards_of,), jnp.float32, low / len(pieces), largest / len(pieces))
        return jnp.repeat(jnp.exp(heights), dims[dim] // shards_of).reshape((-1,) + (1,) * (len(dims) - dim - 1))

    factor_of = one(*pieces[0])
    for cut in pieces[1:]:
        factor_of = factor_of * one(*cut)
    return factor_of


def noise(stream_key, dims, spread, reach, shards=(), held_as=jnp.bfloat16):
    gain = steps_of(stream_key, dims, shards, -0.22, 0.18) if shards else 1.0
    values = jax.random.normal(stream_key, dims, jnp.float32) * spread * gain
    return jnp.minimum(jnp.maximum(values, -reach), reach).astype(held_as)


def setup_inputs(seed: int = 0) -> dict:
    arg_keys = jax.random.split(jax.random.key(seed), 6)
    return {
        "alias_factors": noise(arg_keys[0], (NA * BLK, K), 0.25, 1.5, ((0, 128),)),
        "entity_factors": noise(arg_keys[1], (NE * BLK, K), 0.25, 1.5, ((0, 128),)),
        "tile_ids": draw_tile_ids(jax.random.fold_in(arg_keys[5], 71), 0),
        "tile_score": noise(arg_keys[3], (N_ROW, N_COL, TILES, BLK, BLK), 1.0, 6.0, ((0, 8), (1, 16))),
        "tile_weight": draw_tile_weight(jax.random.fold_in(arg_keys[5], 71), 0),
    }


ridge = 1.0
eps = 1e-6


def tile_terms(alias_t, entity_t, score, weight, own_alias, residual):
    product = jnp.einsum("tak,tek->tae", alias_t.astype(jnp.float32), entity_t.astype(jnp.float32))
    if residual:
        error = weight.astype(jnp.float32) * (score.astype(jnp.float32) - product)
    else:
        error = weight.astype(jnp.float32) * product
    error = error.astype(jnp.bfloat16).astype(jnp.float32)
    if own_alias:
        return jnp.einsum("tae,tek->tak", error, entity_t.astype(jnp.float32))
    return jnp.einsum("tae,tak->tek", error, alias_t.astype(jnp.float32))


def cg_update(x_rows, resid, direction, image, norm_now):
    curve = jnp.sum(direction * image, axis=-1, keepdims=True)
    alpha = norm_now / (curve + eps)
    x_rows = x_rows + alpha * direction
    resid = resid - alpha * image
    norm_next = jnp.sum(resid * resid, axis=-1, keepdims=True)
    direction = resid + (norm_next / (norm_now + eps)) * direction
    return x_rows, resid, direction, norm_next


def reference(alias_factors, entity_factors, tile_ids, tile_score, tile_weight):
    devs = N_ROW * N_COL
    rank = alias_factors.shape[1]
    n_alias = alias_factors.shape[0] // BLK
    n_entity = entity_factors.shape[0] // BLK
    ids = tile_ids.reshape(devs, TILES, 2)
    dev_index = jnp.arange(devs, dtype=jnp.int32)
    row_of = dev_index // N_COL
    col_of = dev_index % N_COL
    alias_glob = (row_of[:, None] * (N_COL * AB_DEV) + ids[:, :, 0]).astype(jnp.int32)
    local_ent = ids[:, :, 1]
    entity_glob = (((local_ent // EB_DEV) * N_COL + col_of[:, None]) * EB_DEV + local_ent % EB_DEV).astype(jnp.int32)
    scores = tile_score.reshape(devs, TILES, BLK, BLK)
    weights = tile_weight.reshape(devs, TILES, BLK, BLK)

    def sweep(alias_blocks, entity_blocks, own_alias, residual):
        count = n_alias if own_alias else n_entity

        def step(total, item):
            a_ids, e_ids, score, weight = item
            terms = tile_terms(alias_blocks[a_ids], entity_blocks[e_ids], score, weight, own_alias, residual)
            target = a_ids if own_alias else e_ids
            return total.at[target].add(terms), None

        total = jnp.zeros((count, BLK, rank), jnp.float32)
        total, _ = lax.scan(step, total, (alias_glob, entity_glob, scores, weights))
        return total.reshape(count * BLK, rank)

    def half(start, alias_blocks, entity_blocks, own_alias):
        x_rows = start.astype(jnp.float32)
        resid = sweep(alias_blocks, entity_blocks, own_alias, True) - ridge * x_rows
        direction = resid
        norm_now = jnp.sum(resid * resid, axis=-1, keepdims=True)
        for step_index in range(2):
            direction_bf = direction.astype(jnp.bfloat16).reshape(-1, BLK, rank)
            if own_alias:
                image = sweep(direction_bf, entity_blocks, True, False)
            else:
                image = sweep(alias_blocks, direction_bf, False, False)
            image = image + ridge * direction
            x_rows, resid, direction, norm_now = cg_update(x_rows, resid, direction, image, norm_now)
        return x_rows.astype(jnp.bfloat16)

    alias_blocks = alias_factors.reshape(n_alias, BLK, rank)
    entity_blocks = entity_factors.reshape(n_entity, BLK, rank)
    alias_new = half(alias_factors, alias_blocks, entity_blocks, True)
    entity_new = half(entity_factors, alias_new.reshape(n_alias, BLK, rank), entity_blocks, False)
    return alias_new, entity_new
```

```python
import functools

import jax
import jax.numpy as jnp
from jax import lax
from jax.experimental import pallas as pl
from jax.experimental.pallas import tpu as pltpu
from jax.sharding import PartitionSpec as P

ridge = 1.0
eps = 1e-06
MESH = pl.DeviceIdType.MESH
F32 = jnp.float32
BF16 = jnp.bfloat16
B = 128
K = 256
T = 96
NB = 16
PAIRS = (T + NB) // 2
STEP = 4

A_TILE, A_OTHER, A_KEY, A_SWAP, A_KEEP, A_LAST = range(6)
E_TILE, E_OTHER, E_KEY, E_KEEP, E_LAST = range(6, 11)


def plan_kernel(ids_ref, out_ref):
    ids = ids_ref[...].astype(F32)
    row_i = lax.broadcasted_iota(jnp.int32, (T, 128), 0).astype(F32)
    lane_i = lax.broadcasted_iota(jnp.int32, (T, 128), 1).astype(F32)
    out_ref[...] = jnp.zeros_like(out_ref)

    def put(row, value):
        out_ref[row : row + 1, :] = value.astype(jnp.int32)

    for key, other, rows in (
        (0, 1, (A_TILE, A_OTHER, A_KEY, A_KEEP, A_LAST)),
        (1, 0, (E_TILE, E_OTHER, E_KEY, E_KEEP, E_LAST)),
    ):
        kc = jnp.broadcast_to(ids[:, key : key + 1], (T, 128))
        oc = jnp.broadcast_to(ids[:, other : other + 1], (T, 128))
        kr = jnp.sum(jnp.where(row_i == lane_i, kc + 1.0, 0.0), axis=0, keepdims=True) - 1.0
        same = jnp.where(kc == kr, 1.0, 0.0)
        rank = jnp.sum(jnp.where(lane_i < row_i, same, 0.0), axis=1, keepdims=True)
        count = jnp.sum(same, axis=1, keepdims=True)
        odd = count - 2.0 * jnp.floor(count * 0.5)
        width = 1.0 + jnp.where(rank == 0.0, odd, 0.0)
        width = jnp.broadcast_to(width, (T, 128))
        n_row = jnp.sum(jnp.where(kc == lane_i, width, 0.0), axis=0, keepdims=True)
        start = jnp.sum(
            jnp.where(lane_i < kc, jnp.broadcast_to(n_row, (T, 128)), 0.0), axis=1, keepdims=True
        )
        pos = jnp.broadcast_to(start + rank, (T, 128))
        hit = jnp.where(pos == lane_i, 1.0, 0.0)
        valid = jnp.sum(hit, axis=0, keepdims=True)
        put(rows[0], jnp.sum(hit * row_i, axis=0, keepdims=True) + T * (1.0 - valid))
        put(rows[1], jnp.sum(hit * oc, axis=0, keepdims=True))
        key_row = jnp.sum(hit * kc, axis=0, keepdims=True)
        put(rows[2], key_row)
        if key == 0:
            high = jnp.floor(key_row * 0.25)
            put(A_SWAP, (key_row - 4.0 * high) * 4.0 + high)
        keep = jnp.where(jnp.broadcast_to(rank, (T, 128)) > 0.0, hit, 0.0)
        put(rows[3], jnp.sum(keep, axis=0, keepdims=True))
        upto = jnp.sum(jnp.where(kc <= lane_i, width, 0.0), axis=0, keepdims=True)
        put(rows[4], upto * 0.5 - 1.0)


class Copies:
    def __init__(self, send, recv):
        self.send, self.recv, self.all = send, recv, []

    def start(self, src, dst, device):
        n = len(self.all)
        cp = pltpu.make_async_remote_copy(
            src_ref=src,
            dst_ref=dst,
            send_sem=self.send.at[n],
            recv_sem=self.recv.at[n],
            device_id=device,
            device_id_type=MESH,
        )
        cp.start()
        self.all.append(cp)
        return cp


N_COPIES = 12 * 4 + 12 * 2 + 7 * 3 + 7 * 2 + 15 + 7


def sweep_kernel(
    plan, x_in, y_in, w_hbm, s_hbm, x_out, y_out,
    w, s, wt, st, xn, run, run_c,
    ga, gb, gy, sa, sb, ra, rb, ta, tb, qa, qb,
    se, me, te, qe, cmsg, emsg, vx, vr, vd, ux, ur, ud,
    send, recv, lsem,
):
    row = lax.axis_index("row")
    col = lax.axis_index("col")
    cy, cc = row // 2, row % 2
    cx, cz = col // 4, col % 4

    def at_x(d):
        return (row, lax.rem(cx + d, 4) * 4 + cz)

    def at_z(d):
        return (row, cx * 4 + lax.rem(cz + d, 4))

    def at_y(d):
        return (lax.rem(cy + d, 4) * 2 + cc, col)

    mate = (cy * 2 + (1 - cc), col)

    copies = Copies(send, recv)
    load_w = pltpu.make_async_copy(w_hbm.at[0, 0], w.at[pl.ds(0, T)], lsem.at[0])
    load_s = pltpu.make_async_copy(s_hbm.at[0, 0], s.at[pl.ds(0, T)], lsem.at[1])
    load_w.start()
    load_s.start()

    barrier = pltpu.get_barrier_semaphore()
    for d in range(1, 16):
        pl.semaphore_signal(barrier, 1, device_id=(row, lax.rem(col + d, 16)), device_id_type=MESH)
    for d in range(1, 8):
        pl.semaphore_signal(barrier, 1, device_id=(lax.rem(row + d, 8), col), device_id_type=MESH)
    pl.semaphore_wait(barrier, 22)

    eye = jnp.where(
        lax.broadcasted_iota(jnp.int32, (B, B), 0) == lax.broadcasted_iota(jnp.int32, (B, B), 1),
        1.0, 0.0,
    ).astype(F32)

    def to_row(column):
        return jnp.sum(jnp.broadcast_to(column, (B, B)) * eye, axis=0, keepdims=True)

    def to_column(line):
        return jnp.sum(jnp.broadcast_to(line, (B, B)) * eye, axis=1, keepdims=True)

    slot_a = cz * 4 + cx
    slot_b = cx * 4 + cz

    def alias_gather(i, value):
        ga[i][slot_a] = value[:, :B]
        gb[i][slot_b] = value[:, B:]
        first_a = [copies.start(ga[i].at[slot_a], ga[i].at[slot_a], at_x(d)) for d in (1, 3, 2)]
        first_b = [copies.start(gb[i].at[slot_b], gb[i].at[slot_b], at_z(d)) for d in (1, 3, 2)]

        def middle():
            for cp in first_a:
                cp.wait_recv()
            rows_a = pl.ds(cz * 4, 4)
            second = [copies.start(ga[i].at[rows_a], ga[i].at[rows_a], at_z(d)) for d in (1, 3, 2)]
            for cp in first_b:
                cp.wait_recv()
            rows_b = pl.ds(cx * 4, 4)
            second += [copies.start(gb[i].at[rows_b], gb[i].at[rows_b], at_x(d)) for d in (1, 3, 2)]
            return second

        return middle

    def finish(second):
        for cp in second:
            cp.wait_recv()

    def alias_spread(i):
        for b in range(NB):
            block = run[plan[A_LAST, b] + 1]
            sa[i, (b % 4) * 4 + b // 4] = block[:, :B].astype(BF16)
            sb[i, b] = block[:, B:].astype(BF16)
        first_a, first_b = [], []
        for n, d in enumerate((1, 3, 2)):
            rows_a = pl.ds(lax.rem(cz + d, 4) * 4, 4)
            first_a.append(copies.start(sa.at[i, rows_a], ra.at[i, n], at_z(d)))
            rows_b = pl.ds(lax.rem(cx + d, 4) * 4, 4)
            first_b.append(copies.start(sb.at[i, rows_b], rb.at[i, n], at_x(d)))

        def middle():
            second = []
            for first, sx, rx, tx, qx, base, own, at in (
                (first_a, sa, ra, ta, qa, cz * 4, cx, at_x),
                (first_b, sb, rb, tb, qb, cx * 4, cz, at_z),
            ):
                for cp in first:
                    cp.wait_recv()
                for n, d in enumerate((1, 3, 2)):
                    j = lax.rem(own + d, 4)
                    total = sx[i, base + j].astype(F32)
                    for m in range(3):
                        total = total + rx[i, m, j].astype(F32)
                    tx[i, n] = total
                    second.append(copies.start(tx.at[i, n], qx.at[i, n], at(d)))
            return second

        def end(second):
            finish(second)
            halves = []
            for sx, rx, qx, base, own in (
                (sa, ra, qa, cz * 4, cx), (sb, rb, qb, cx * 4, cz),
            ):
                total = sx[i, base + own].astype(F32)
                for m in range(3):
                    total = total + rx[i, m, own].astype(F32)
                for m in range(3):
                    total = total + qx[i, m]
                halves.append(total)
            return jnp.concatenate(halves, axis=1)

        return middle, end

    def entity_gather(i, values=None):
        own = pl.ds(row * 2, 2)
        for n in range(2):
            gy[i][row * 2 + n] = values[n]
        first = [copies.start(gy[i].at[own], gy[i].at[own], at_y(d)) for d in (1, 3, 2)]
        second = [copies.start(gy[i].at[own], gy[i].at[own], mate)]

        def middle():
            for cp, d in zip(first, (1, 3, 2)):
                cp.wait_recv()
                came = pl.ds((lax.rem(cy + 4 - d, 4) * 2 + cc) * 2, 2)
                second.append(copies.start(gy[i].at[came], gy[i].at[came], mate))
            return second

        return middle

    def entity_spread(i):
        for e in range(NB):
            owner = e // 2
            se[i, (owner % 2) * 4 + owner // 2, e % 2] = run[plan[E_LAST, e] + 1]
        first = []
        for n, d in enumerate((1, 3, 2, 0)):
            there = (1 - cc) * 4 + lax.rem(cy + d, 4)
            first.append(copies.start(se.at[i, there], me.at[i, n], mate))

        def middle():
            second = []
            for n, d in enumerate((1, 3, 2)):
                first[n].wait_recv()
                here = cc * 4 + lax.rem(cy + d, 4)
                for m in range(2):
                    te[i, n, m] = (se[i, here, m] + me[i, n, m]).astype(BF16)
                second.append(copies.start(te.at[i, n], qe.at[i, n], at_y(d)))
            first[3].wait_recv()
            return second

        def end(second):
            finish(second)
            here = cc * 4 + cy
            parts = []
            for m in range(2):
                total = se[i, here, m] + me[i, 3, m]
                for n in range(3):
                    total = total + qe[i, n, m].astype(F32)
                parts.append(total)
            return parts

        return middle, end

    nt = (((1,), (1,)), ((), ()))
    nn = (((1,), (0,)), ((), ()))

    def tiles(load_row, load_pair, wx, sx, rows, mode):
        tile_row, keep_row = rows

        def body(q, carry):
            weights, products, pairs = [], [], []
            for u in range(STEP):
                p = q * STEP + u
                mine = load_row(2 * p)
                pair = load_pair(p)
                products.append(lax.dot_general(mine, pair, nt, preferred_element_type=F32))
                pairs.append(pair)
            errors = []
            for u in range(STEP):
                p = q * STEP + u
                t0, t1 = plan[tile_row, 2 * p], plan[tile_row, 2 * p + 1]
                weight = jnp.concatenate([wx[t0], wx[t1]], axis=1).astype(F32)
                if mode == "resid":
                    score = jnp.concatenate([sx[t0], sx[t1]], axis=1).astype(F32)
                    errors.append((weight * (score - products[u])).astype(BF16))
                elif mode == "image":
                    errors.append((weight * products[u]).astype(BF16))
                else:
                    errors.append(weight * products[u] * products[u])
            for u in range(STEP):
                p = q * STEP + u
                keep = plan[keep_row, 2 * p].astype(F32)
                if mode == "curve":
                    term = errors[u][:, :B] + errors[u][:, B:]
                    run_c[p + 1] = run_c[p] * keep + term
                else:
                    term = lax.dot_general(errors[u], pairs[u], nn, preferred_element_type=F32)
                    run[p + 1] = run[p] * keep + term
            return carry

        lax.fori_loop(0, PAIRS // STEP, body, 0)

    def alias_tiles(i, mode):
        def load_row(n):
            return jnp.concatenate([ga[i][plan[A_SWAP, n]], gb[i][plan[A_KEY, n]]], axis=1)

        def load_pair(p):
            e0, e1 = plan[A_OTHER, 2 * p], plan[A_OTHER, 2 * p + 1]
            return jnp.concatenate([gy[0][e0], gy[0][e1]], axis=0)

        tiles(load_row, load_pair, w, s, (A_TILE, A_KEEP), mode)

    def entity_tiles(i, mode):
        def load_row(n):
            return gy[i][plan[E_KEY, n]]

        def load_pair(p):
            a0, a1 = plan[E_OTHER, 2 * p], plan[E_OTHER, 2 * p + 1]
            return jnp.concatenate([xn[a0], xn[a1]], axis=0)

        tiles(load_row, load_pair, wt, st, (E_TILE, E_KEEP), mode)

    def flip(source, target, low, high):
        def body(n, carry):
            for u in range(2):
                target[low + 2 * n + u] = source[low + 2 * n + u].T
            return carry

        lax.fori_loop(0, (high - low) // 2, body, 0)

    def curve_row(last):
        block = run_c[last + 1]
        high = block.astype(BF16)
        low = (block - high.astype(F32)).astype(BF16)
        ones = jnp.ones((16, B), BF16)
        total = lax.dot_general(ones, high, nt, preferred_element_type=F32)
        total = total + lax.dot_general(ones, low, nt, preferred_element_type=F32)
        return total[0:1]

    def first_step(x, r, image_of):
        d = r
        rr = jnp.sum(r * r, axis=-1, keepdims=True)
        image = image_of + ridge * d
        step = rr / (jnp.sum(d * image, axis=-1, keepdims=True) + eps)
        x = x + step * d
        r = r - step * image
        new = jnp.sum(r * r, axis=-1, keepdims=True)
        d = r + (new / (rr + eps)) * d
        return x, d, new

    x0 = x_in[...]
    mid_x = alias_gather(0, x0)
    mid_y = entity_gather(0, [y_in[pl.ds(0, B), :], y_in[pl.ds(B, B), :]])
    zero = jnp.zeros((B, B), BF16)
    for ref in (w, s, wt, st):
        ref[T] = zero
    run[0] = jnp.zeros((B, K), F32)
    run_c[0] = jnp.zeros((B, B), F32)
    second_x = mid_x()
    second_y = mid_y()
    load_w.wait()
    load_s.wait()
    flip(w, wt, 0, 32)
    finish(second_x)
    finish(second_y)
    alias_tiles(0, "resid")
    middle, end = alias_spread(0)
    flip(w, wt, 32, 64)
    second = middle()
    image = end(second)
    vx[...] = x_in[...].astype(F32)
    vr[...] = image - ridge * vx[...]
    mid = alias_gather(1, vr[...].astype(BF16))
    second = mid()
    flip(w, wt, 64, 96)
    finish(second)
    alias_tiles(1, "image")
    middle, end = alias_spread(1)
    flip(s, st, 0, 32)
    second = middle()
    image = end(second)
    x1, d1, rr1 = first_step(vx[...], vr[...], image)
    vd[...] = d1
    vx[...] = x1
    own_rr = to_row(rr1)
    own_dd = ridge * to_row(jnp.sum(d1 * d1, axis=-1, keepdims=True))
    mid = alias_gather(2, vd[...].astype(BF16))
    second = mid()
    mid_x = alias_gather(3, vx[...].astype(BF16))
    flip(s, st, 32, 64)
    finish(second)
    second_x = mid_x()
    alias_tiles(2, "curve")
    for b in range(NB):
        line = curve_row(plan[A_LAST, b])
        cmsg[col, pl.ds(b, 1), :] = line + jnp.where(col == b, own_dd, 0.0)
    cmsg[col, pl.ds(NB, 8), :] = jnp.broadcast_to(own_rr, (8, B))
    small = [
        copies.start(cmsg.at[col], cmsg.at[col], (row, lax.rem(col + d, 16))) for d in range(1, 16)
    ]
    flip(s, st, 64, 96)
    finish(second_x)
    finish(small)
    total = cmsg[0, pl.ds(0, NB), :]
    for b in range(1, NB):
        total = total + cmsg[b, pl.ds(0, NB), :]
    for b in range(NB):
        step = to_column(cmsg[b, pl.ds(NB, 1), :] / (total[b : b + 1] + eps))
        a_slot = (b % 4) * 4 + b // 4
        left = ga[3][a_slot].astype(F32) + step * ga[2][a_slot].astype(F32)
        right = gb[3][b].astype(F32) + step * gb[2][b].astype(F32)
        xn[b] = jnp.concatenate([left, right], axis=1).astype(BF16)
    mine = jnp.sum(
        jnp.where(lax.broadcasted_iota(jnp.int32, (NB, B), 0) == col, total, 0.0),
        axis=0, keepdims=True,
    )
    step = to_column(cmsg[col, pl.ds(NB, 1), :] / (mine + eps))
    x_out[...] = (vx[...] + step * vd[...]).astype(BF16)

    entity_tiles(0, "resid")
    middle, end = entity_spread(0)
    second = middle()
    parts = end(second)
    for m in range(2):
        ux[m] = y_in[pl.ds(m * B, B), :].astype(F32)
        ur[m] = parts[m] - ridge * ux[m]
    mid = entity_gather(1, [ur[m].astype(BF16) for m in range(2)])
    finish(mid())
    entity_tiles(1, "image")
    middle, end = entity_spread(1)
    second = middle()
    parts = end(second)
    norms, dots = [], []
    for m in range(2):
        y1, d1, rr1 = first_step(ux[m], ur[m], parts[m])
        ux[m] = y1
        ud[m] = d1
        norms.append(rr1)
        dots.append(ridge * jnp.sum(d1 * d1, axis=-1, keepdims=True))
    mid = entity_gather(2, [ud[m].astype(BF16) for m in range(2)])
    finish(mid())
    entity_tiles(2, "curve")
    for e in range(NB):
        emsg[0, e // 2, pl.ds(e % 2, 1), :] = curve_row(plan[E_LAST, e])
    small = []
    for d in range(1, 8):
        there = lax.rem(row + d, 8)
        small.append(copies.start(emsg.at[0, there], emsg.at[1, row], (there, col)))
    emsg[1, row] = emsg[0, row]
    finish(small)
    total = emsg[1, 0]
    for n in range(1, 8):
        total = total + emsg[1, n]
    for m in range(2):
        step = norms[m] / (to_column(total[m : m + 1]) + dots[m] + eps)
        y_out[pl.ds(m * B, B), :] = (ux[m] + step * ud[m]).astype(BF16)
    for cp in copies.all:
        cp.wait_send()


def on_device(alias_factors, entity_factors, tile_ids, tile_score, tile_weight):
    plan = pl.pallas_call(
        plan_kernel,
        name="tile_plan",
        out_shape=jax.ShapeDtypeStruct((16, 128), jnp.int32),
    )(tile_ids.reshape(T, 2))
    vmem = pl.BlockSpec(memory_space=pltpu.VMEM)
    hbm = pl.BlockSpec(memory_space=pl.ANY)
    V = pltpu.VMEM
    return pl.pallas_call(
        sweep_kernel,
        name="als_sweep",
        out_shape=(
            jax.ShapeDtypeStruct((B, K), BF16),
            jax.ShapeDtypeStruct((2 * B, K), BF16),
        ),
        in_specs=[pl.BlockSpec(memory_space=pltpu.SMEM), vmem, vmem, hbm, hbm],
        out_specs=(vmem, vmem),
        scratch_shapes=[
            V((T + 1, B, B), BF16), V((T + 1, B, B), BF16),
            V((T + 1, B, B), BF16), V((T + 1, B, B), BF16),
            V((NB, B, K), BF16),
            V((PAIRS + 1, B, K), F32), V((PAIRS + 1, B, B), F32),
            [V((NB, B, B), BF16)] * 4, [V((NB, B, B), BF16)] * 4, [V((NB, B, K), BF16)] * 3,
            V((2, NB, B, B), BF16), V((2, NB, B, B), BF16),
            V((2, 3, 4, B, B), BF16), V((2, 3, 4, B, B), BF16),
            V((2, 3, B, B), F32), V((2, 3, B, B), F32),
            V((2, 3, B, B), F32), V((2, 3, B, B), F32),
            V((2, 8, 2, B, K), F32), V((2, 4, 2, B, K), F32),
            V((2, 3, 2, B, K), BF16), V((2, 3, 2, B, K), BF16),
            V((NB, NB + 8, B), F32), V((2, 8, 8, B), F32),
            V((B, K), F32), V((B, K), F32), V((B, K), F32),
            V((2, B, K), F32), V((2, B, K), F32), V((2, B, K), F32),
            pltpu.SemaphoreType.DMA((N_COPIES,)),
            pltpu.SemaphoreType.DMA((N_COPIES,)),
            pltpu.SemaphoreType.DMA((2,)),
        ],
        compiler_params=pltpu.CompilerParams(
            collective_id=0, has_side_effects=True, vmem_limit_bytes=60 * 2**20
        ),
    )(plan, alias_factors, entity_factors, tile_weight, tile_score)


def solution(mesh):
    placed = (
        P(("row", "col"), None),
        P(("row", "col"), None),
        P("row", "col", None, None),
        P("row", "col", None, None, None),
        P("row", "col", None, None, None),
    )
    return jax.shard_map(
        on_device,
        mesh=mesh,
        in_specs=placed,
        out_specs=(P(("row", "col"), None), P(("row", "col"), None)),
        check_vma=False,
    )
```

```python
import functools

import jax
import jax.numpy as jnp
from jax import lax
from jax.experimental import pallas as pl
from jax.experimental.pallas import tpu as pltpu
from jax.sharding import PartitionSpec as P

ridge = 1.0
eps = 1e-06
MESH = pl.DeviceIdType.MESH
F32 = jnp.float32
BF16 = jnp.bfloat16
B = 128
K = 256
T = 96
NB = 16
PAIRS = (T + NB) // 2
STEP = 28
NS = 2
R = B // NS
CHUNKS = ((0, 4),)
PRE = True
THROTTLE = False

A_TILE, A_OTHER, A_KEY, A_SWAP, A_KEEP, A_LAST = range(6)
E_TILE, E_OTHER, E_KEY, E_KEEP, E_LAST = range(6, 11)


def plan_kernel(ids_ref, out_ref):
    ids = ids_ref[...].astype(F32)
    row_i = lax.broadcasted_iota(jnp.int32, (T, 128), 0).astype(F32)
    lane_i = lax.broadcasted_iota(jnp.int32, (T, 128), 1).astype(F32)
    row_t = lax.broadcasted_iota(jnp.int32, (T, T), 0).astype(F32)
    lane_t = lax.broadcasted_iota(jnp.int32, (T, T), 1).astype(F32)
    col = lax.axis_index("col")
    cx, cz = (col // 4).astype(F32), (col % 4).astype(F32)
    out_ref[...] = jnp.zeros_like(out_ref)

    def put(row, value):
        out_ref[row : row + 1, :] = value.astype(jnp.int32)

    lines = [jnp.broadcast_to(ids[n : n + 1, :], (T, T)) for n in range(2)]
    columns = [
        jnp.sum(jnp.where(row_t == lane_t, line, 0.0), axis=1, keepdims=True) for line in lines
    ]
    for key, rows in (
        (0, (A_TILE, A_OTHER, A_KEY, A_KEEP, A_LAST)),
        (1, (E_TILE, E_OTHER, E_KEY, E_KEEP, E_LAST)),
    ):
        kc = jnp.broadcast_to(columns[key], (T, 128))
        oc = jnp.broadcast_to(columns[1 - key], (T, 128))
        same = jnp.where(jnp.broadcast_to(columns[key], (T, T)) == lines[key], 1.0, 0.0)
        rank = jnp.sum(jnp.where(lane_t < row_t, same, 0.0), axis=1, keepdims=True)
        count = jnp.sum(same, axis=1, keepdims=True)
        odd = count - 2.0 * jnp.floor(count * 0.5)
        width = jnp.broadcast_to(1.0 + jnp.where(rank == 0.0, odd, 0.0), (T, 128))
        n_row = jnp.sum(jnp.where(kc == lane_i, width, 0.0), axis=0, keepdims=True)
        start = jnp.sum(
            jnp.where(lane_i < kc, jnp.broadcast_to(n_row, (T, 128)), 0.0), axis=1, keepdims=True
        )
        pos = jnp.broadcast_to(start + rank, (T, 128))
        hit = jnp.where(pos == lane_i, 1.0, 0.0)
        valid = jnp.sum(hit, axis=0, keepdims=True)
        put(rows[0], jnp.sum(hit * row_i, axis=0, keepdims=True) + T * (1.0 - valid))
        put(rows[1], jnp.sum(hit * oc, axis=0, keepdims=True))
        key_row = jnp.sum(hit * kc, axis=0, keepdims=True)
        if key == 0:
            high = jnp.floor(key_row * 0.25)
            low = key_row - 4.0 * high
            put(A_KEY, high * 4.0 + low - cz + jnp.where(low < cz, 4.0, 0.0))
            put(A_SWAP, low * 4.0 + high - cx + jnp.where(high < cx, 4.0, 0.0))
        else:
            put(rows[2], key_row)
        keep = jnp.where(jnp.broadcast_to(rank, (T, 128)) > 0.0, hit, 0.0)
        put(rows[3], jnp.sum(keep, axis=0, keepdims=True))
        upto = jnp.sum(jnp.where(kc <= lane_i, width, 0.0), axis=0, keepdims=True)
        put(rows[4], upto * 0.5 - 1.0)


class Copies:
    def __init__(self, send, recv):
        self.send, self.recv, self.all, self.done, self.batch = send, recv, [], [], []

    def start(self, src, dst, device):
        n = len(self.all)
        cp = pltpu.make_async_remote_copy(
            src_ref=src,
            dst_ref=dst,
            send_sem=self.send.at[n],
            recv_sem=self.recv.at[n],
            device_id=device,
            device_id_type=MESH,
        )
        cp.start()
        self.all.append(cp)
        return cp

    def flush(self, some):
        for cp in some:
            if not any(cp is other for other in self.done):
                cp.wait_send()
                self.done.append(cp)

    def turn(self, batch):
        if THROTTLE:
            self.flush(self.batch)
        self.batch = batch
        return batch


N_GATHER = 18 if PRE else 12
N_COPIES = NS * (N_GATHER * 4 + (6 * len(CHUNKS) + 6) * 2 + 7 * 2 + 7 * 2) + 7 + 15 + 7
FAR = (1, 3, 2)


def sweep_kernel(
    plan, x_in, y_in, w_hbm, s_hbm, x_out, y_out,
    w, s, wt, st, xn, run, run_c, ga, gb, gy0, gy, sa, sb, ra, rb, ta, tb, qa, qb,
    se, me, te, qe, cmsg, emsg, vx, vr, vd, vn, vq, ux, ur, ud, un, uq,
    send, recv, lsem,
):
    row = lax.axis_index("row")
    col = lax.axis_index("col")
    cy, cc = row // 2, row % 2
    cx, cz = col // 4, col % 4

    def at_x(d):
        return (row, lax.rem(cx + d, 4) * 4 + cz)

    def at_z(d):
        return (row, cx * 4 + lax.rem(cz + d, 4))

    def at_y(d):
        return (lax.rem(cy + d, 4) * 2 + cc, col)

    mate = (cy * 2 + (1 - cc), col)

    copies = Copies(send, recv)
    load_w = pltpu.make_async_copy(w_hbm.at[0, 0], w.at[pl.ds(0, T)], lsem.at[0])
    load_s = pltpu.make_async_copy(s_hbm.at[0, 0], s.at[pl.ds(0, T)], lsem.at[1])
    load_w.start()
    load_s.start()

    barrier = pltpu.get_barrier_semaphore()
    for d in range(1, 16):
        pl.semaphore_signal(barrier, 1, device_id=(row, lax.rem(col + d, 16)), device_id_type=MESH)
    for d in range(1, 8):
        pl.semaphore_signal(barrier, 1, device_id=(lax.rem(row + d, 8), col), device_id_type=MESH)
    pl.semaphore_wait(barrier, 22)

    eye = jnp.where(
        lax.broadcasted_iota(jnp.int32, (B, B), 0) == lax.broadcasted_iota(jnp.int32, (B, B), 1),
        1.0, 0.0,
    ).astype(F32)

    def to_row(column):
        return jnp.sum(jnp.broadcast_to(column, (B, B)) * eye, axis=0, keepdims=True)

    def to_column(line):
        return jnp.sum(jnp.broadcast_to(line, (B, B)) * eye, axis=1, keepdims=True)

    def arrived(list_of_copies):
        for cp in list_of_copies:
            cp.wait_recv()

    def alias_gather(i, h, value):
        a, b = ga[i][h], gb[i][h]
        a[cz * 4] = value[:, :B]
        b[cx * 4] = value[:, B:]
        first_a, first_b, second = [], [], []
        for d in FAR:
            first_a.append(copies.start(a.at[cz * 4], a.at[cz * 4 + 4 - d], at_x(d)))
            first_b.append(copies.start(b.at[cx * 4], b.at[cx * 4 + 4 - d], at_z(d)))
        if PRE:
            for d in FAR:
                second.append(copies.start(a.at[cz * 4], a.at[cz * 4], at_z(d)))
                second.append(copies.start(b.at[cx * 4], b.at[cx * 4], at_x(d)))
        skip = 1 if PRE else 0

        def middle():
            arrived(first_a + first_b)
            batch = copies.turn([])
            for ref, base, at in ((a, cz * 4, at_z), (b, cx * 4, at_x)):
                rows = pl.ds(base + skip, 4 - skip)
                for d in FAR:
                    batch.append(copies.start(ref.at[rows], ref.at[rows], at(d)))
            return second + batch

        return middle

    def alias_spread(i, h):
        halves = (
            (sa[i][h], ra[i][h], ta[i][h], qa[i][h], cx, cz, at_x, at_z),
            (sb[i][h], rb[i][h], tb[i][h], qb[i][h], cz, cx, at_z, at_x),
        )
        firsts = [[], []]
        for low, high in CHUNKS:
            for k, (sx, rx, tx, qx, near, far, at_near, at_far) in enumerate(halves):
                for m in range(4):
                    for pos in range(low, high):
                        other = lax.rem(near + 3 - pos, 4)
                        block = other * 4 + m if k == 0 else m * 4 + other
                        part = run[plan[A_LAST, block] + 1, h * R : (h + 1) * R, k * B : (k + 1) * B]
                        sx[m, pos] = part.astype(BF16)
            batch = copies.turn([])
            for k, (sx, rx, tx, qx, near, far, at_near, at_far) in enumerate(halves):
                span = pl.ds(low, high - low)
                firsts[k].append(
                    [
                        copies.start(sx.at[lax.rem(far + d, 4), span], rx.at[n, span], at_far(d))
                        for n, d in enumerate(FAR)
                    ]
                )
                batch.extend(firsts[k][-1])

        def middle():
            second = []
            for c, (low, high) in enumerate(CHUNKS):
                for k, (sx, rx, tx, qx, near, far, at_near, at_far) in enumerate(halves):
                    arrived(firsts[k][c])
                    for pos in range(low, min(high, 3)):
                        total = sx[far, pos].astype(F32)
                        for n in range(3):
                            total = total + rx[n, pos].astype(F32)
                        tx[pos] = total.astype(BF16)
                        second.append(copies.start(tx.at[pos], qx.at[pos], at_near(3 - pos)))
            return second

        def end(second):
            arrived(second)
            sums = []
            for sx, rx, tx, qx, near, far, at_near, at_far in halves:
                total = sx[far, 3].astype(F32)
                for n in range(3):
                    total = total + rx[n, 3].astype(F32)
                for n in range(3):
                    total = total + qx[n].astype(F32)
                sums.append(total)
            return jnp.concatenate(sums, axis=1)

        return middle, end

    def entity_gather(ref, values):
        own = pl.ds(row * 2, 2)
        for n in range(2):
            ref[row * 2 + n] = values[n]
        first = copies.turn([])
        first.extend([copies.start(ref.at[own], ref.at[own], at_y(d)) for d in FAR])
        second = [copies.start(ref.at[own], ref.at[own], mate)]

        def middle():
            for cp, d in zip(first, FAR):
                cp.wait_recv()
                came = pl.ds((lax.rem(cy + 4 - d, 4) * 2 + cc) * 2, 2)
                second.append(copies.start(ref.at[came], ref.at[came], mate))
            return second

        return middle

    def entity_spread(i, h):
        sx, mx, tx, qx = se[i][h], me[i][h], te[i][h], qe[i][h]
        first = []
        for n, d in enumerate(FAR + (0,)):
            y = lax.rem(cy + d, 4)
            for c in range(2):
                for m in range(2):
                    sx[c, n, m] = run[plan[E_LAST, (y * 2 + c) * 2 + m] + 1, h * R : (h + 1) * R]
            first.append(copies.start(sx.at[1 - cc, n], mx.at[n], mate))

        def middle():
            second = copies.turn([])
            for n, d in enumerate(FAR):
                first[n].wait_recv()
                for m in range(2):
                    tx[n, m] = (sx[cc, n, m] + mx[n, m]).astype(BF16)
                second.append(copies.start(tx.at[n], qx.at[n], at_y(d)))
            first[3].wait_recv()
            return second

        def end(second):
            arrived(second)
            parts = []
            for m in range(2):
                total = sx[cc, 3, m] + mx[3, m]
                for n in range(3):
                    total = total + qx[n, m].astype(F32)
                parts.append(total)
            return parts

        return middle, end

    nt = (((1,), (1,)), ((), ()))
    nn = (((1,), (0,)), ((), ()))

    def tiles(load_row, load_pair, wx, sx, rows, mode):
        tile_row, keep_row = rows

        def body(q, carry):
            products, pairs, errors = [], [], []
            for u in range(STEP):
                p = q * STEP + u
                mine = load_row(2 * p)
                pair = load_pair(p)
                products.append(lax.dot_general(mine, pair, nt, preferred_element_type=F32))
                pairs.append(pair)
            for u in range(STEP):
                p = q * STEP + u
                t0, t1 = plan[tile_row, 2 * p], plan[tile_row, 2 * p + 1]
                weight = jnp.concatenate([wx[t0], wx[t1]], axis=1).astype(F32)
                if mode == "resid":
                    score = jnp.concatenate([sx[t0], sx[t1]], axis=1).astype(F32)
                    errors.append((weight * (score - products[u])).astype(BF16))
                elif mode == "image":
                    errors.append((weight * products[u]).astype(BF16))
                else:
                    errors.append(weight * products[u] * products[u])
            for u in range(STEP):
                p = q * STEP + u
                keep = plan[keep_row, 2 * p].astype(F32)
                if mode == "curve":
                    term = errors[u][:, :B] + errors[u][:, B:]
                    run_c[p + 1] = run_c[p] * keep + term
                else:
                    term = lax.dot_general(errors[u], pairs[u], nn, preferred_element_type=F32)
                    run[p + 1] = run[p] * keep + term
            return carry

        lax.fori_loop(0, PAIRS // STEP, body, 0)

    def alias_tiles(i, mode):
        def load_row(n):
            left = jnp.concatenate([ga[i][h][plan[A_SWAP, n]] for h in range(NS)], axis=0)
            right = jnp.concatenate([gb[i][h][plan[A_KEY, n]] for h in range(NS)], axis=0)
            return jnp.concatenate([left, right], axis=1)

        def load_pair(p):
            e0, e1 = plan[A_OTHER, 2 * p], plan[A_OTHER, 2 * p + 1]
            return jnp.concatenate([gy0[e0], gy0[e1]], axis=0)

        tiles(load_row, load_pair, w, s, (A_TILE, A_KEEP), mode)

    def entity_tiles(i, mode):
        def load_row(n):
            if i == 0:
                return gy0[plan[E_KEY, n]]
            return jnp.concatenate([gy[i - 1][h][plan[E_KEY, n]] for h in range(NS)], axis=0)

        def load_pair(p):
            a0, a1 = plan[E_OTHER, 2 * p], plan[E_OTHER, 2 * p + 1]
            return jnp.concatenate([xn[a0], xn[a1]], axis=0)

        tiles(load_row, load_pair, wt, st, (E_TILE, E_KEEP), mode)

    def flip(source, target, low, high):
        def body(n, carry):
            for u in range(4):
                target[low + 4 * n + u] = source[low + 4 * n + u].T
            return carry

        lax.fori_loop(0, (high - low) // 4, body, 0)

    def curve_row(last):
        block = run_c[last + 1]
        high = block.astype(BF16)
        low = (block - high.astype(F32)).astype(BF16)
        ones = jnp.ones((16, B), BF16)
        total = lax.dot_general(ones, high, nt, preferred_element_type=F32)
        total = total + lax.dot_general(ones, low, nt, preferred_element_type=F32)
        return total[0:1]

    def first_step(x, r, image_of):
        d = r
        rr = jnp.sum(r * r, axis=-1, keepdims=True)
        image = image_of + ridge * d
        step = rr / (jnp.sum(d * image, axis=-1, keepdims=True) + eps)
        x = x + step * d
        r = r - step * image
        new = jnp.sum(r * r, axis=-1, keepdims=True)
        d = r + (new / (rr + eps)) * d
        return x, d, new

    flips = [
        (src, dst, n, n + 16) for src, dst in ((w, wt), (s, st)) for n in range(0, T, 16)
    ]

    def together(streams):
        streams = list(streams)
        while streams:
            for stream in list(streams):
                try:
                    next(stream)
                except StopIteration:
                    streams.remove(stream)

    def gap():
        for n in range(3):
            if flips:
                flip(*flips.pop(0))

    y_gather = []

    def alias_stream(h):
        rows = pl.ds(h * R, R)
        x0 = x_in[rows, :]
        mid = alias_gather(0, h, x0)
        if h == 0:
            mid_y = entity_gather(gy0, [y_in[pl.ds(0, B), :], y_in[pl.ds(B, B), :]])
        yield
        second = mid()
        if h == 0:
            y_gather.append(mid_y())
            load_w.wait()
            load_s.wait()
            zero = jnp.zeros((B, B), BF16)
            for ref in (w, s, wt, st):
                ref[T] = zero
            run[0] = jnp.zeros((B, K), F32)
            run_c[0] = jnp.zeros((B, B), F32)
        if h == NS - 1:
            gap()
        yield
        arrived(second)
        if h == NS - 1:
            arrived(y_gather[0])
            alias_tiles(0, "resid")
        yield
        middle, end = alias_spread(0, h)
        if h == NS - 1:
            gap()
        yield
        second = middle()
        yield
        image = end(second)
        x = x_in[rows, :].astype(F32)
        r = image - ridge * x
        vr[rows, :] = r
        mid = alias_gather(1, h, r.astype(BF16))
        yield
        second = mid()
        if h == NS - 1:
            gap()
        yield
        arrived(second)
        if h == NS - 1:
            alias_tiles(1, "image")
        yield
        middle, end = alias_spread(1, h)
        if h == NS - 1:
            gap()
        yield
        second = middle()
        yield
        image = end(second)
        x1, d1, rr1 = first_step(x_in[rows, :].astype(F32), vr[rows, :], image)
        mid = alias_gather(2, h, d1.astype(BF16))
        vd[rows, :] = d1
        vx[rows, :] = x1
        vn[rows, :] = jnp.broadcast_to(rr1, (R, B))
        vq[rows, :] = jnp.broadcast_to(ridge * jnp.sum(d1 * d1, axis=-1, keepdims=True), (R, B))
        yield
        second = mid()
        if h == NS - 1:
            gap()
        yield
        mid_x = alias_gather(3, h, vx[rows, :].astype(BF16))
        arrived(second)
        yield
        x_gather.extend(mid_x())
        if h == NS - 1:
            alias_tiles(2, "curve")

    x_gather = []
    together([alias_stream(h) for h in range(NS)])
    while flips:
        flip(*flips.pop(0))
    own_dd = jnp.sum(vq[...] * eye, axis=0, keepdims=True)
    own_rr = jnp.sum(vn[...] * eye, axis=0, keepdims=True)
    for b in range(NB):
        line = curve_row(plan[A_LAST, b])
        cmsg[col, pl.ds(b, 1), :] = line + jnp.where(col == b, own_dd, 0.0)
    cmsg[col, pl.ds(NB, 8), :] = jnp.broadcast_to(own_rr, (8, B))
    small = [
        copies.start(cmsg.at[col], cmsg.at[col], (row, lax.rem(col + d, 16))) for d in range(1, 16)
    ]
    arrived(x_gather)
    arrived(small)
    total = cmsg[0, pl.ds(0, NB), :]
    for b in range(1, NB):
        total = total + cmsg[b, pl.ds(0, NB), :]
    for b in range(NB):
        step = to_column(cmsg[b, pl.ds(NB, 1), :] / (total[b : b + 1] + eps))
        a_slot = (b % 4) * 4 + lax.rem(b // 4 + 4 - cx, 4)
        b_slot = (b // 4) * 4 + lax.rem(b % 4 + 4 - cz, 4)
        for h in range(NS):
            cut = slice(h * R, (h + 1) * R)
            left = ga[3][h][a_slot].astype(F32) + step[cut] * ga[2][h][a_slot].astype(F32)
            right = gb[3][h][b_slot].astype(F32) + step[cut] * gb[2][h][b_slot].astype(F32)
            xn[b, cut] = jnp.concatenate([left, right], axis=1).astype(BF16)

    def entity_stream(h):
        halves = [pl.ds(m * B + h * R, R) for m in range(2)]
        if h == 0:
            entity_tiles(0, "resid")
        middle, end = entity_spread(0, h)
        yield
        second = middle()
        yield
        parts = end(second)
        rs = [parts[m] - ridge * y_in[halves[m], :].astype(F32) for m in range(2)]
        mid = entity_gather(gy[0][h], [r.astype(BF16) for r in rs])
        for m in range(2):
            ur[halves[m], :] = rs[m]
        yield
        second = mid()
        yield
        arrived(second)
        if h == NS - 1:
            entity_tiles(1, "image")
        yield
        middle, end = entity_spread(1, h)
        yield
        second = middle()
        yield
        parts = end(second)
        steps = [
            first_step(y_in[halves[m], :].astype(F32), ur[halves[m], :], parts[m])
            for m in range(2)
        ]
        mid = entity_gather(gy[1][h], [step[1].astype(BF16) for step in steps])
        for m, (y1, d1, rr1) in enumerate(steps):
            ux[halves[m], :] = y1
            ud[halves[m], :] = d1
            un[halves[m], :] = jnp.broadcast_to(rr1, (R, B))
            uq[halves[m], :] = jnp.broadcast_to(
                ridge * jnp.sum(d1 * d1, axis=-1, keepdims=True), (R, B)
            )
        yield
        second = mid()
        yield
        arrived(second)
        if h == NS - 1:
            entity_tiles(2, "curve")

    together([entity_stream(h) for h in range(NS)])
    for e in range(NB):
        emsg[0, e // 2, pl.ds(e % 2, 1), :] = curve_row(plan[E_LAST, e])
    small = []
    for d in range(1, 8):
        there = lax.rem(row + d, 8)
        small.append(copies.start(emsg.at[0, there], emsg.at[1, row], (there, col)))
    emsg[1, row] = emsg[0, row]
    mine = jnp.sum(
        jnp.where(lax.broadcasted_iota(jnp.int32, (NB, B), 0) == col, total, 0.0),
        axis=0, keepdims=True,
    )
    step = to_column(cmsg[col, pl.ds(NB, 1), :] / (mine + eps))
    x_out[...] = (vx[...] + step * vd[...]).astype(BF16)
    arrived(small)
    total = emsg[1, 0]
    for n in range(1, 8):
        total = total + emsg[1, n]
    for m in range(2):
        rows = pl.ds(m * B, B)
        step = un[rows, :][:, :1] / (to_column(total[m : m + 1]) + uq[rows, :][:, :1] + eps)
        y_out[rows, :] = (ux[rows, :] + step * ud[rows, :]).astype(BF16)
    copies.flush(copies.all)


def emit_kernel(x_in, y_in, x_out, y_out):
    x_out[...] = x_in[...]
    y_out[...] = y_in[...]


def on_device(alias_factors, entity_factors, tile_ids, tile_score, tile_weight):
    plan = pl.pallas_call(
        plan_kernel,
        name="tile_plan",
        out_shape=jax.ShapeDtypeStruct((16, 128), jnp.int32),
    )(tile_ids[0, 0].T)
    vmem = pl.BlockSpec(memory_space=pltpu.VMEM)
    hbm = pl.BlockSpec(memory_space=pl.ANY)
    V = pltpu.VMEM

    def each(n, shape, dtype):
        return [[V(shape, dtype) for h in range(NS)] for i in range(n)]

    results = pl.pallas_call(
        sweep_kernel,
        name="als_sweep",
        out_shape=(
            jax.ShapeDtypeStruct((B, K), BF16),
            jax.ShapeDtypeStruct((2 * B, K), BF16),
        ),
        in_specs=[pl.BlockSpec(memory_space=pltpu.SMEM), vmem, vmem, hbm, hbm],
        out_specs=(vmem, vmem),
        scratch_shapes=[
            V((T + 1, B, B), BF16), V((T + 1, B, B), BF16),
            V((T + 1, B, B), BF16), V((T + 1, B, B), BF16),
            V((NB, B, K), BF16),
            V((PAIRS + 1, B, K), F32), V((PAIRS + 1, B, B), F32),
            each(4, (NB, R, B), BF16), each(4, (NB, R, B), BF16),
            V((NB, B, K), BF16), each(2, (NB, R, K), BF16),
            each(2, (4, 4, R, B), BF16), each(2, (4, 4, R, B), BF16),
            each(2, (3, 4, R, B), BF16), each(2, (3, 4, R, B), BF16),
            each(2, (3, R, B), BF16), each(2, (3, R, B), BF16),
            each(2, (3, R, B), BF16), each(2, (3, R, B), BF16),
            each(2, (2, 4, 2, R, K), F32), each(2, (4, 2, R, K), F32),
            each(2, (3, 2, R, K), BF16), each(2, (3, 2, R, K), BF16),
            V((NB, NB + 8, B), F32), V((2, 8, 8, B), F32),
            V((B, K), F32), V((B, K), F32), V((B, K), F32), V((B, B), F32), V((B, B), F32),
            V((2 * B, K), F32), V((2 * B, K), F32), V((2 * B, K), F32),
            V((2 * B, B), F32), V((2 * B, B), F32),
            pltpu.SemaphoreType.DMA((N_COPIES,)),
            pltpu.SemaphoreType.DMA((N_COPIES,)),
            pltpu.SemaphoreType.DMA((2,)),
        ],
        compiler_params=pltpu.CompilerParams(
            collective_id=0, has_side_effects=True, vmem_limit_bytes=60 * 2**20
        ),
    )(plan, alias_factors, entity_factors, tile_weight, tile_score)
    return pl.pallas_call(
        emit_kernel,
        name="emit",
        out_shape=(
            jax.ShapeDtypeStruct((B, K), BF16),
            jax.ShapeDtypeStruct((2 * B, K), BF16),
        ),
    )(*results)


def solution(mesh):
    placed = (
        P(("row", "col"), None),
        P(("row", "col"), None),
        P("row", "col", None, None),
        P("row", "col", None, None, None),
        P("row", "col", None, None, None),
    )
    return jax.shard_map(
        on_device,
        mesh=mesh,
        in_specs=placed,
        out_specs=(P(("row", "col"), None), P(("row", "col"), None)),
        check_vma=False,
    )
```

```python
import functools

import jax
import jax.numpy as jnp
from jax import lax
from jax.experimental import pallas as pl
from jax.experimental.pallas import tpu as pltpu
from jax.sharding import PartitionSpec as P

ridge = 1.0
eps = 1e-06
MESH = pl.DeviceIdType.MESH
F32 = jnp.float32
BF16 = jnp.bfloat16
B = 128
K = 256
T = 96
NB = 16
PAIRS = (T + NB) // 2
STEP = 28
NS = 2
R = B // NS
CHUNKS = ((0, 4),)
PRE = True

A_TILE, A_OTHER, A_KEY, A_SWAP, A_KEEP, A_LAST = range(6)
E_TILE, E_OTHER, E_KEY, E_KEEP, E_LAST = range(6, 11)
TOPS = (T, 15, 15, 15, 1, PAIRS - 1, T, 15, 15, 1, PAIRS - 1)


def tile_plan(ids_ref, out_ref, cx, cz):
    ids = ids_ref[...].astype(F32)
    row_i = lax.broadcasted_iota(jnp.int32, (T, 128), 0).astype(F32)
    lane_i = lax.broadcasted_iota(jnp.int32, (T, 128), 1).astype(F32)
    row_t = lax.broadcasted_iota(jnp.int32, (T, T), 0).astype(F32)
    lane_t = lax.broadcasted_iota(jnp.int32, (T, T), 1).astype(F32)
    cx, cz = cx.astype(F32), cz.astype(F32)
    out_ref[...] = jnp.zeros_like(out_ref)

    def put(row, value):
        top = TOPS[row]
        out_ref[row : row + 1, :] = jnp.minimum(jnp.maximum(value.astype(jnp.int32), 0), top)

    lines = [jnp.broadcast_to(ids[n : n + 1, :], (T, T)) for n in range(2)]
    columns = [
        jnp.sum(jnp.where(row_t == lane_t, line, 0.0), axis=1, keepdims=True) for line in lines
    ]
    for key, rows in (
        (0, (A_TILE, A_OTHER, A_KEY, A_KEEP, A_LAST)),
        (1, (E_TILE, E_OTHER, E_KEY, E_KEEP, E_LAST)),
    ):
        kc = jnp.broadcast_to(columns[key], (T, 128))
        oc = jnp.broadcast_to(columns[1 - key], (T, 128))
        same = jnp.where(jnp.broadcast_to(columns[key], (T, T)) == lines[key], 1.0, 0.0)
        rank = jnp.sum(jnp.where(lane_t < row_t, same, 0.0), axis=1, keepdims=True)
        count = jnp.sum(same, axis=1, keepdims=True)
        odd = count - 2.0 * jnp.floor(count * 0.5)
        width = jnp.broadcast_to(1.0 + jnp.where(rank == 0.0, odd, 0.0), (T, 128))
        n_row = jnp.sum(jnp.where(kc == lane_i, width, 0.0), axis=0, keepdims=True)
        start = jnp.sum(
            jnp.where(lane_i < kc, jnp.broadcast_to(n_row, (T, 128)), 0.0), axis=1, keepdims=True
        )
        pos = jnp.broadcast_to(start + rank, (T, 128))
        hit = jnp.where(pos == lane_i, 1.0, 0.0)
        valid = jnp.sum(hit, axis=0, keepdims=True)
        put(rows[0], jnp.sum(hit * row_i, axis=0, keepdims=True) + T * (1.0 - valid))
        put(rows[1], jnp.sum(hit * oc, axis=0, keepdims=True))
        key_row = jnp.sum(hit * kc, axis=0, keepdims=True)
        if key == 0:
            high = jnp.floor(key_row * 0.25)
            low = key_row - 4.0 * high
            put(A_KEY, high * 4.0 + low - cz + jnp.where(low < cz, 4.0, 0.0))
            put(A_SWAP, low * 4.0 + high - cx + jnp.where(high < cx, 4.0, 0.0))
        else:
            put(rows[2], key_row)
        keep = jnp.where(jnp.broadcast_to(rank, (T, 128)) > 0.0, hit, 0.0)
        put(rows[3], jnp.sum(keep, axis=0, keepdims=True))
        upto = jnp.sum(jnp.where(kc <= lane_i, width, 0.0), axis=0, keepdims=True)
        put(rows[4], upto * 0.5 - 1.0)


class Copies:
    def __init__(self, send, recv):
        self.send, self.recv, self.all, self.done, self.batch = send, recv, [], [], []

    def start(self, src, dst, device):
        n = len(self.all)
        cp = pltpu.make_async_remote_copy(
            src_ref=src,
            dst_ref=dst,
            send_sem=self.send.at[n],
            recv_sem=self.recv.at[n],
            device_id=device,
            device_id_type=MESH,
        )
        cp.start()
        self.all.append(cp)
        return cp

    def flush(self, some):
        for cp in some:
            if not any(cp is other for other in self.done):
                cp.wait_send()
                self.done.append(cp)


N_GATHER = 18 if PRE else 12
N_COPIES = NS * (N_GATHER * 4 + (6 * len(CHUNKS) + 6) * 2 + 7 * 2 + 7 * 2) + 7 + 6 + 4
FAR = (1, 3, 2)


def sweep_kernel(
    ids, x_in, y_in, w_hbm, s_hbm, x_out, y_out,
    w, s, wt, st, xn, run, run_c, ga, gb, gy0, gy, sa, sb, ra, rb, ta, tb, qa, qb,
    se, me, te, qe, cmsg, csum, emsg, ecome, esum, elast, vx, vr, vd, vn, vq, ux, ur, ud, un, uq,
    plan_v, plan, send, recv, lsem,
):
    row = lax.axis_index("row")
    col = lax.axis_index("col")
    cy, cc = row // 2, row % 2
    cx, cz = col // 4, col % 4

    def at_x(d):
        return (row, lax.rem(cx + d, 4) * 4 + cz)

    def at_z(d):
        return (row, cx * 4 + lax.rem(cz + d, 4))

    def at_y(d):
        return (lax.rem(cy + d, 4) * 2 + cc, col)

    mate = (cy * 2 + (1 - cc), col)

    copies = Copies(send, recv)
    load_w = pltpu.make_async_copy(w_hbm.at[0, 0], w.at[pl.ds(0, T)], lsem.at[0])
    load_s = pltpu.make_async_copy(s_hbm.at[0, 0], s.at[pl.ds(0, T)], lsem.at[1])
    load_plan = pltpu.make_async_copy(plan_v, plan, lsem.at[2])
    load_w.start()
    load_s.start()

    barrier = pltpu.get_barrier_semaphore()
    for peer in [at(d) for at in (at_x, at_z, at_y) for d in FAR] + [mate]:
        pl.semaphore_signal(barrier, 1, device_id=peer, device_id_type=MESH)
    pl.semaphore_wait(barrier, 10)

    eye = jnp.where(
        lax.broadcasted_iota(jnp.int32, (B, B), 0) == lax.broadcasted_iota(jnp.int32, (B, B), 1),
        1.0, 0.0,
    ).astype(F32)

    def to_row(column):
        return jnp.sum(jnp.broadcast_to(column, (B, B)) * eye, axis=0, keepdims=True)

    def to_column(line):
        return jnp.sum(jnp.broadcast_to(line, (B, B)) * eye, axis=1, keepdims=True)

    def arrived(list_of_copies):
        for cp in list_of_copies:
            cp.wait_recv()

    def alias_gather(i, h, value):
        a, b = ga[i][h], gb[i][h]
        a[cz * 4] = value[:, :B]
        b[cx * 4] = value[:, B:]
        first_a, first_b, second = [], [], []
        for d in FAR:
            first_a.append(copies.start(a.at[cz * 4], a.at[cz * 4 + 4 - d], at_x(d)))
            first_b.append(copies.start(b.at[cx * 4], b.at[cx * 4 + 4 - d], at_z(d)))
        if PRE:
            for d in FAR:
                second.append(copies.start(a.at[cz * 4], a.at[cz * 4], at_z(d)))
                second.append(copies.start(b.at[cx * 4], b.at[cx * 4], at_x(d)))
        skip = 1 if PRE else 0

        def middle():
            arrived(first_a + first_b)
            batch = []
            for ref, base, at in ((a, cz * 4, at_z), (b, cx * 4, at_x)):
                rows = pl.ds(base + skip, 4 - skip)
                for d in FAR:
                    batch.append(copies.start(ref.at[rows], ref.at[rows], at(d)))
            return second + batch

        return middle

    def alias_spread(i, h):
        halves = (
            (sa[i][h], ra[i][h], ta[i][h], qa[i][h], cx, cz, at_x, at_z),
            (sb[i][h], rb[i][h], tb[i][h], qb[i][h], cz, cx, at_z, at_x),
        )
        firsts = [[], []]
        for low, high in CHUNKS:
            for k, (sx, rx, tx, qx, near, far, at_near, at_far) in enumerate(halves):
                for m in range(4):
                    for pos in range(low, high):
                        other = lax.rem(near + 3 - pos, 4)
                        block = other * 4 + m if k == 0 else m * 4 + other
                        part = run[plan[A_LAST, block] + 1, h * R : (h + 1) * R, k * B : (k + 1) * B]
                        sx[m, pos] = part.astype(BF16)
                span = pl.ds(low, high - low)
                firsts[k].append(
                    [
                        copies.start(sx.at[lax.rem(far + d, 4), span], rx.at[n, span], at_far(d))
                        for n, d in enumerate(FAR)
                    ]
                )

        def middle():
            second = []
            for c, (low, high) in enumerate(CHUNKS):
                for k, (sx, rx, tx, qx, near, far, at_near, at_far) in enumerate(halves):
                    arrived(firsts[k][c])
                    for pos in range(low, min(high, 3)):
                        total = sx[far, pos].astype(F32)
                        for n in range(3):
                            total = total + rx[n, pos].astype(F32)
                        tx[pos] = total
                        second.append(copies.start(tx.at[pos], qx.at[pos], at_near(3 - pos)))
            return second

        def end(second):
            arrived(second)
            sums = []
            for sx, rx, tx, qx, near, far, at_near, at_far in halves:
                total = sx[far, 3].astype(F32)
                for n in range(3):
                    total = total + rx[n, 3].astype(F32)
                for n in range(3):
                    total = total + qx[n]
                sums.append(total)
            return jnp.concatenate(sums, axis=1)

        return middle, end

    def entity_gather(ref, values):
        own = pl.ds(row * 2, 2)
        for n in range(2):
            ref[row * 2 + n] = values[n]
        first = []
        first.extend([copies.start(ref.at[own], ref.at[own], at_y(d)) for d in FAR])
        second = [copies.start(ref.at[own], ref.at[own], mate)]

        def middle():
            for cp, d in zip(first, FAR):
                cp.wait_recv()
                came = pl.ds((lax.rem(cy + 4 - d, 4) * 2 + cc) * 2, 2)
                second.append(copies.start(ref.at[came], ref.at[came], mate))
            return second

        return middle

    def entity_spread(i, h):
        sx, mx, tx, qx = se[i][h], me[i][h], te[i][h], qe[i][h]
        first = []
        for n, d in enumerate(FAR + (0,)):
            y = lax.rem(cy + d, 4)
            for c in range(2):
                for m in range(2):
                    sx[c, n, m] = run[plan[E_LAST, (y * 2 + c) * 2 + m] + 1, h * R : (h + 1) * R]
            first.append(copies.start(sx.at[1 - cc, n], mx.at[n], mate))

        def middle():
            second = []
            for n, d in enumerate(FAR):
                first[n].wait_recv()
                for m in range(2):
                    tx[n, m] = (sx[cc, n, m] + mx[n, m]).astype(BF16)
                second.append(copies.start(tx.at[n], qx.at[n], at_y(d)))
            first[3].wait_recv()
            return second

        def end(second):
            arrived(second)
            parts = []
            for m in range(2):
                total = sx[cc, 3, m] + mx[3, m]
                for n in range(3):
                    total = total + qx[n, m].astype(F32)
                parts.append(total)
            return parts

        return middle, end

    nt = (((1,), (1,)), ((), ()))
    nn = (((1,), (0,)), ((), ()))

    def tiles(load_row, load_pair, wx, sx, rows, mode):
        tile_row, keep_row = rows

        def body(q, carry):
            products, pairs, errors = [], [], []
            for u in range(STEP):
                p = q * STEP + u
                mine = load_row(2 * p)
                pair = load_pair(p)
                products.append(lax.dot_general(mine, pair, nt, preferred_element_type=F32))
                pairs.append(pair)
            for u in range(STEP):
                p = q * STEP + u
                t0, t1 = plan[tile_row, 2 * p], plan[tile_row, 2 * p + 1]
                weight = jnp.concatenate([wx[t0], wx[t1]], axis=1).astype(F32)
                if mode == "resid":
                    score = jnp.concatenate([sx[t0], sx[t1]], axis=1).astype(F32)
                    errors.append((weight * (score - products[u])).astype(BF16))
                elif mode == "image":
                    errors.append((weight * products[u]).astype(BF16))
                else:
                    errors.append(weight * products[u] * products[u])
            for u in range(STEP):
                p = q * STEP + u
                keep = plan[keep_row, 2 * p].astype(F32)
                if mode == "curve":
                    term = errors[u][:, :B] + errors[u][:, B:]
                    run_c[p + 1] = run_c[p] * keep + term
                else:
                    term = lax.dot_general(errors[u], pairs[u], nn, preferred_element_type=F32)
                    run[p + 1] = run[p] * keep + term
            return carry

        lax.fori_loop(0, PAIRS // STEP, body, 0)

    def alias_tiles(i, mode):
        def load_row(n):
            left = jnp.concatenate([ga[i][h][plan[A_SWAP, n]] for h in range(NS)], axis=0)
            right = jnp.concatenate([gb[i][h][plan[A_KEY, n]] for h in range(NS)], axis=0)
            return jnp.concatenate([left, right], axis=1)

        def load_pair(p):
            e0, e1 = plan[A_OTHER, 2 * p], plan[A_OTHER, 2 * p + 1]
            return jnp.concatenate([gy0[e0], gy0[e1]], axis=0)

        tiles(load_row, load_pair, w, s, (A_TILE, A_KEEP), mode)

    def entity_tiles(i, mode):
        def load_row(n):
            if i == 0:
                return gy0[plan[E_KEY, n]]
            return jnp.concatenate([gy[i - 1][h][plan[E_KEY, n]] for h in range(NS)], axis=0)

        def load_pair(p):
            a0, a1 = plan[E_OTHER, 2 * p], plan[E_OTHER, 2 * p + 1]
            return jnp.concatenate([xn[a0], xn[a1]], axis=0)

        tiles(load_row, load_pair, wt, st, (E_TILE, E_KEEP), mode)

    def flip(source, target, low, high):
        def body(n, carry):
            for u in range(4):
                target[low + 4 * n + u] = source[low + 4 * n + u].T
            return carry

        lax.fori_loop(0, (high - low) // 4, body, 0)

    def curve_row(last):
        block = run_c[last + 1]
        high = block.astype(BF16)
        low = (block - high.astype(F32)).astype(BF16)
        ones = jnp.ones((16, B), BF16)
        total = lax.dot_general(ones, high, nt, preferred_element_type=F32)
        total = total + lax.dot_general(ones, low, nt, preferred_element_type=F32)
        return total[0:1]

    def first_step(x, r, image_of):
        d = r
        rr = jnp.sum(r * r, axis=-1, keepdims=True)
        image = image_of + ridge * d
        step = rr / (jnp.sum(d * image, axis=-1, keepdims=True) + eps)
        x = x + step * d
        r = r - step * image
        new = jnp.sum(r * r, axis=-1, keepdims=True)
        d = r + (new / (rr + eps)) * d
        return x, d, new

    flips = [
        (src, dst, n, n + 16) for src, dst in ((w, wt), (s, st)) for n in range(0, T, 16)
    ]

    def together(streams):
        streams = list(streams)
        while streams:
            for stream in list(streams):
                try:
                    next(stream)
                except StopIteration:
                    streams.remove(stream)

    def gap():
        for n in range(3):
            if flips:
                flip(*flips.pop(0))

    y_gather = []

    def alias_stream(h):
        rows = pl.ds(h * R, R)
        x0 = x_in[rows, :]
        mid = alias_gather(0, h, x0)
        if h == 0:
            mid_y = entity_gather(gy0, [y_in[pl.ds(0, B), :], y_in[pl.ds(B, B), :]])
        yield
        second = mid()
        if h == 0:
            tile_plan(ids, plan_v, cx, cz)
            load_plan.start()
            y_gather.append(mid_y())
            load_plan.wait()
            load_w.wait()
            load_s.wait()
            zero = jnp.zeros((B, B), BF16)
            for ref in (w, s, wt, st):
                ref[T] = zero
            run[0] = jnp.zeros((B, K), F32)
            run_c[0] = jnp.zeros((B, B), F32)
            emsg[...] = jnp.zeros_like(emsg)
        if h == NS - 1:
            gap()
        yield
        arrived(second)
        if h == NS - 1:
            arrived(y_gather[0])
            alias_tiles(0, "resid")
        yield
        middle, end = alias_spread(0, h)
        if h == NS - 1:
            gap()
        yield
        second = middle()
        yield
        image = end(second)
        x = x_in[rows, :].astype(F32)
        r = image - ridge * x
        vr[rows, :] = r
        mid = alias_gather(1, h, r.astype(BF16))
        yield
        second = mid()
        if h == NS - 1:
            gap()
        yield
        arrived(second)
        if h == NS - 1:
            alias_tiles(1, "image")
        yield
        middle, end = alias_spread(1, h)
        if h == NS - 1:
            gap()
        yield
        second = middle()
        yield
        image = end(second)
        x1, d1, rr1 = first_step(x_in[rows, :].astype(F32), vr[rows, :], image)
        mid = alias_gather(2, h, d1.astype(BF16))
        vd[rows, :] = d1
        vx[rows, :] = x1
        vn[rows, :] = jnp.broadcast_to(rr1, (R, B))
        vq[rows, :] = jnp.broadcast_to(ridge * jnp.sum(d1 * d1, axis=-1, keepdims=True), (R, B))
        yield
        second = mid()
        if h == NS - 1:
            gap()
        yield
        mid_x = alias_gather(3, h, vx[rows, :].astype(BF16))
        arrived(second)
        yield
        x_gather.extend(mid_x())
        if h == NS - 1:
            alias_tiles(2, "curve")

    x_gather = []
    together([alias_stream(h) for h in range(NS)])
    while flips:
        flip(*flips.pop(0))
    own_dd = jnp.sum(vq[...] * eye, axis=0, keepdims=True)
    own_rr = jnp.sum(vn[...] * eye, axis=0, keepdims=True)
    for b in range(NB):
        line = curve_row(plan[A_LAST, b])
        cmsg[0, pl.ds(b, 1), :] = line + jnp.where(col == b, own_dd, 0.0)
        cmsg[0, pl.ds(NB + b, 1), :] = jnp.where(col == b, own_rr, 0.0)
    arrived([copies.start(cmsg.at[0], cmsg.at[4 - d], at_x(d)) for d in FAR])
    csum[0] = (cmsg[0] + cmsg[1]) + (cmsg[2] + cmsg[3])
    small = [copies.start(csum.at[0], csum.at[4 - d], at_z(d)) for d in FAR]
    arrived(x_gather)
    arrived(small)
    total = (csum[0] + csum[1]) + (csum[2] + csum[3])
    rates = total[NB:] / (total[:NB] + eps)
    for b in range(NB):
        step = to_column(rates[b : b + 1])
        a_slot = (b % 4) * 4 + lax.rem(b // 4 + 4 - cx, 4)
        b_slot = (b // 4) * 4 + lax.rem(b % 4 + 4 - cz, 4)
        for h in range(NS):
            cut = slice(h * R, (h + 1) * R)
            left = ga[3][h][a_slot].astype(F32) + step[cut] * ga[2][h][a_slot].astype(F32)
            right = gb[3][h][b_slot].astype(F32) + step[cut] * gb[2][h][b_slot].astype(F32)
            xn[b, cut] = jnp.concatenate([left, right], axis=1).astype(BF16)

    def entity_stream(h):
        halves = [pl.ds(m * B + h * R, R) for m in range(2)]
        if h == 0:
            entity_tiles(0, "resid")
        middle, end = entity_spread(0, h)
        yield
        second = middle()
        yield
        parts = end(second)
        rs = [parts[m] - ridge * y_in[halves[m], :].astype(F32) for m in range(2)]
        mid = entity_gather(gy[0][h], [r.astype(BF16) for r in rs])
        for m in range(2):
            ur[halves[m], :] = rs[m]
        yield
        second = mid()
        yield
        arrived(second)
        if h == NS - 1:
            entity_tiles(1, "image")
        yield
        middle, end = entity_spread(1, h)
        yield
        second = middle()
        yield
        parts = end(second)
        steps = [
            first_step(y_in[halves[m], :].astype(F32), ur[halves[m], :], parts[m])
            for m in range(2)
        ]
        mid = entity_gather(gy[1][h], [step[1].astype(BF16) for step in steps])
        for m, (y1, d1, rr1) in enumerate(steps):
            ux[halves[m], :] = y1
            ud[halves[m], :] = d1
            un[halves[m], :] = jnp.broadcast_to(rr1, (R, B))
            uq[halves[m], :] = jnp.broadcast_to(
                ridge * jnp.sum(d1 * d1, axis=-1, keepdims=True), (R, B)
            )
        yield
        second = mid()
        yield
        arrived(second)
        if h == NS - 1:
            entity_tiles(2, "curve")

    together([entity_stream(h) for h in range(NS)])
    for n, d in enumerate(FAR + (0,)):
        y = lax.rem(cy + d, 4)
        for c in range(2):
            for m in range(2):
                emsg[c, n, m : m + 1] = curve_row(plan[E_LAST, (y * 2 + c) * 2 + m])
    first = copies.start(emsg.at[1 - cc], ecome, mate)
    mine = jnp.sum(
        jnp.where(lax.broadcasted_iota(jnp.int32, (NB, B), 0) == col, rates, 0.0),
        axis=0, keepdims=True,
    )
    x_out[...] = (vx[...] + to_column(mine) * vd[...]).astype(BF16)
    arrived([first])
    small = []
    for n, d in enumerate(FAR):
        esum[n] = emsg[cc, n] + ecome[n]
        small.append(copies.start(esum.at[n], elast.at[n], at_y(d)))
    total = emsg[cc, 3] + ecome[3]
    arrived(small)
    for n in range(3):
        total = total + elast[n]
    for m in range(2):
        rows = pl.ds(m * B, B)
        step = un[rows, :][:, :1] / (to_column(total[m : m + 1]) + uq[rows, :][:, :1] + eps)
        y_out[rows, :] = (ux[rows, :] + step * ud[rows, :]).astype(BF16)
    copies.flush(copies.all)


def emit_kernel(x_in, y_in, x_out, y_out):
    x_out[...] = x_in[...]
    y_out[...] = y_in[...]


def on_device(alias_factors, entity_factors, tile_ids, tile_score, tile_weight):
    vmem = pl.BlockSpec(memory_space=pltpu.VMEM)
    hbm = pl.BlockSpec(memory_space=pl.ANY)
    V = pltpu.VMEM

    def each(n, shape, dtype):
        return [[V(shape, dtype) for h in range(NS)] for i in range(n)]

    results = pl.pallas_call(
        sweep_kernel,
        name="als_sweep",
        out_shape=(
            jax.ShapeDtypeStruct((B, K), BF16),
            jax.ShapeDtypeStruct((2 * B, K), BF16),
        ),
        in_specs=[vmem, vmem, vmem, hbm, hbm],
        out_specs=(vmem, vmem),
        scratch_shapes=[
            V((T + 1, B, B), BF16), V((T + 1, B, B), BF16),
            V((T + 1, B, B), BF16), V((T + 1, B, B), BF16),
            V((NB, B, K), BF16),
            V((PAIRS + 1, B, K), F32), V((PAIRS + 1, B, B), F32),
            each(4, (NB, R, B), BF16), each(4, (NB, R, B), BF16),
            V((NB, B, K), BF16), each(2, (NB, R, K), BF16),
            each(2, (4, 4, R, B), BF16), each(2, (4, 4, R, B), BF16),
            each(2, (3, 4, R, B), BF16), each(2, (3, 4, R, B), BF16),
            each(2, (3, R, B), F32), each(2, (3, R, B), F32),
            each(2, (3, R, B), F32), each(2, (3, R, B), F32),
            each(2, (2, 4, 2, R, K), F32), each(2, (4, 2, R, K), F32),
            each(2, (3, 2, R, K), BF16), each(2, (3, 2, R, K), BF16),
            V((4, 2 * NB, B), F32), V((4, 2 * NB, B), F32),
            V((2, 4, 8, B), F32), V((4, 8, B), F32), V((3, 8, B), F32), V((3, 8, B), F32),
            V((B, K), F32), V((B, K), F32), V((B, K), F32), V((B, B), F32), V((B, B), F32),
            V((2 * B, K), F32), V((2 * B, K), F32), V((2 * B, K), F32),
            V((2 * B, B), F32), V((2 * B, B), F32),
            V((16, 128), jnp.int32), pltpu.SMEM((16, 128), jnp.int32),
            pltpu.SemaphoreType.DMA((N_COPIES,)),
            pltpu.SemaphoreType.DMA((N_COPIES,)),
            pltpu.SemaphoreType.DMA((3,)),
        ],
        compiler_params=pltpu.CompilerParams(
            collective_id=0, has_side_effects=True, vmem_limit_bytes=60 * 2**20
        ),
    )(tile_ids[0, 0].T, alias_factors, entity_factors, tile_weight, tile_score)
    return pl.pallas_call(
        emit_kernel,
        name="emit",
        out_shape=(
            jax.ShapeDtypeStruct((B, K), BF16),
            jax.ShapeDtypeStruct((2 * B, K), BF16),
        ),
    )(*results)


def solution(mesh):
    placed = (
        P(("row", "col"), None),
        P(("row", "col"), None),
        P("row", "col", None, None),
        P("row", "col", None, None, None),
        P("row", "col", None, None, None),
    )
    return jax.shard_map(
        on_device,
        mesh=mesh,
        in_specs=placed,
        out_specs=(P(("row", "col"), None), P(("row", "col"), None)),
        check_vma=False,
    )
```

```python
import functools

import jax
import jax.numpy as jnp
from jax import lax
from jax.experimental import pallas as pl
from jax.experimental.pallas import tpu as pltpu
from jax.sharding import PartitionSpec as P

ridge = 1.0
eps = 1e-06
MESH = pl.DeviceIdType.MESH
F32 = jnp.float32
BF16 = jnp.bfloat16
B = 128
K = 256
T = 96
NB = 16
PAIRS = (T + NB) // 2
STEP = 28
NS = 2
R = B // NS
CHUNKS = ((0, 4),)
PRE = True

A_TILE, A_OTHER, A_KEY, A_SWAP, A_KEEP, A_LAST = range(6)
E_TILE, E_OTHER, E_KEY, E_KEEP, E_LAST = range(6, 11)
TOPS = (T, 15, 15, 15, 1, PAIRS - 1, T, 15, 15, 1, PAIRS - 1)


def tile_plan(ids_ref, out_ref, cx, cz):
    ids = ids_ref[...].astype(F32)
    row_i = lax.broadcasted_iota(jnp.int32, (T, 128), 0).astype(F32)
    lane_i = lax.broadcasted_iota(jnp.int32, (T, 128), 1).astype(F32)
    row_t = lax.broadcasted_iota(jnp.int32, (T, T), 0).astype(F32)
    lane_t = lax.broadcasted_iota(jnp.int32, (T, T), 1).astype(F32)
    cx, cz = cx.astype(F32), cz.astype(F32)
    out_ref[...] = jnp.zeros_like(out_ref)

    def put(row, value):
        top = TOPS[row]
        out_ref[row : row + 1, :] = jnp.minimum(jnp.maximum(value.astype(jnp.int32), 0), top)

    lines = [jnp.broadcast_to(ids[n : n + 1, :], (T, T)) for n in range(2)]
    columns = [
        jnp.sum(jnp.where(row_t == lane_t, line, 0.0), axis=1, keepdims=True) for line in lines
    ]
    for key, rows in (
        (0, (A_TILE, A_OTHER, A_KEY, A_KEEP, A_LAST)),
        (1, (E_TILE, E_OTHER, E_KEY, E_KEEP, E_LAST)),
    ):
        kc = jnp.broadcast_to(columns[key], (T, 128))
        oc = jnp.broadcast_to(columns[1 - key], (T, 128))
        same = jnp.where(jnp.broadcast_to(columns[key], (T, T)) == lines[key], 1.0, 0.0)
        rank = jnp.sum(jnp.where(lane_t < row_t, same, 0.0), axis=1, keepdims=True)
        count = jnp.sum(same, axis=1, keepdims=True)
        odd = count - 2.0 * jnp.floor(count * 0.5)
        width = jnp.broadcast_to(1.0 + jnp.where(rank == 0.0, odd, 0.0), (T, 128))
        n_row = jnp.sum(jnp.where(kc == lane_i, width, 0.0), axis=0, keepdims=True)
        start = jnp.sum(
            jnp.where(lane_i < kc, jnp.broadcast_to(n_row, (T, 128)), 0.0), axis=1, keepdims=True
        )
        pos = jnp.broadcast_to(start + rank, (T, 128))
        hit = jnp.where(pos == lane_i, 1.0, 0.0)
        valid = jnp.sum(hit, axis=0, keepdims=True)
        put(rows[0], jnp.sum(hit * row_i, axis=0, keepdims=True) + T * (1.0 - valid))
        put(rows[1], jnp.sum(hit * oc, axis=0, keepdims=True))
        key_row = jnp.sum(hit * kc, axis=0, keepdims=True)
        if key == 0:
            high = jnp.floor(key_row * 0.25)
            low = key_row - 4.0 * high
            put(A_KEY, high * 4.0 + low - cz + jnp.where(low < cz, 4.0, 0.0))
            put(A_SWAP, low * 4.0 + high - cx + jnp.where(high < cx, 4.0, 0.0))
        else:
            put(rows[2], key_row)
        keep = jnp.where(jnp.broadcast_to(rank, (T, 128)) > 0.0, hit, 0.0)
        put(rows[3], jnp.sum(keep, axis=0, keepdims=True))
        upto = jnp.sum(jnp.where(kc <= lane_i, width, 0.0), axis=0, keepdims=True)
        put(rows[4], upto * 0.5 - 1.0)


class Copies:
    def __init__(self, send, recv):
        self.send, self.recv, self.all, self.done, self.batch = send, recv, [], [], []

    def start(self, src, dst, device):
        n = len(self.all)
        cp = pltpu.make_async_remote_copy(
            src_ref=src,
            dst_ref=dst,
            send_sem=self.send.at[n],
            recv_sem=self.recv.at[n],
            device_id=device,
            device_id_type=MESH,
        )
        cp.start()
        self.all.append(cp)
        return cp

    def flush(self, some):
        for cp in some:
            if not any(cp is other for other in self.done):
                cp.wait_send()
                self.done.append(cp)


N_GATHER = 18 if PRE else 12
N_COPIES = NS * (N_GATHER * 4 + (6 * len(CHUNKS) + 6) * 2 + 7 * 2 + 7 * 2) + 7 + 6 + 4
FAR = (1, 3, 2)


def sweep_kernel(
    ids, x_hbm, y_hbm, w_hbm, s_hbm, x_out, y_out,
    w, s, wt, st, xn, run, run_c, ga, gb, gy0, gy, sa, sb, ra, rb, ta, tb, qa, qb,
    se, me, te, qe, cmsg, csum, emsg, ecome, esum, elast, vx, vr, vd, vn, vq, ux, ur, ud, un, uq,
    x_in, y_in, plan_v, plan, send, recv, lsem,
):
    row = lax.axis_index("row")
    col = lax.axis_index("col")
    cy, cc = row // 2, row % 2
    cx, cz = col // 4, col % 4

    def at_x(d):
        return (row, lax.rem(cx + d, 4) * 4 + cz)

    def at_z(d):
        return (row, cx * 4 + lax.rem(cz + d, 4))

    def at_y(d):
        return (lax.rem(cy + d, 4) * 2 + cc, col)

    mate = (cy * 2 + (1 - cc), col)

    copies = Copies(send, recv)
    load_w = pltpu.make_async_copy(w_hbm.at[0, 0], w.at[pl.ds(0, T)], lsem.at[0])
    load_s = pltpu.make_async_copy(s_hbm.at[0, 0], s.at[pl.ds(0, T)], lsem.at[1])
    load_plan = pltpu.make_async_copy(plan_v, plan, lsem.at[2])
    load_x = pltpu.make_async_copy(x_hbm, x_in, lsem.at[3])
    load_y = pltpu.make_async_copy(y_hbm, y_in, lsem.at[4])
    load_x.start()
    load_y.start()

    barrier = pltpu.get_barrier_semaphore()
    for peer in [at(d) for at in (at_x, at_z, at_y) for d in FAR] + [mate]:
        pl.semaphore_signal(barrier, 1, device_id=peer, device_id_type=MESH)
    pl.semaphore_wait(barrier, 10)

    eye = jnp.where(
        lax.broadcasted_iota(jnp.int32, (B, B), 0) == lax.broadcasted_iota(jnp.int32, (B, B), 1),
        1.0, 0.0,
    ).astype(F32)

    def to_row(column):
        return jnp.sum(jnp.broadcast_to(column, (B, B)) * eye, axis=0, keepdims=True)

    def to_column(line):
        return jnp.sum(jnp.broadcast_to(line, (B, B)) * eye, axis=1, keepdims=True)

    def arrived(list_of_copies):
        for cp in list_of_copies:
            cp.wait_recv()

    load_x.wait()
    load_y.wait()

    def alias_gather(i, h, value):
        a, b = ga[i][h], gb[i][h]
        a[cz * 4] = value[:, :B]
        b[cx * 4] = value[:, B:]
        first_a, first_b, second = [], [], []
        for d in FAR:
            first_a.append(copies.start(a.at[cz * 4], a.at[cz * 4 + 4 - d], at_x(d)))
            first_b.append(copies.start(b.at[cx * 4], b.at[cx * 4 + 4 - d], at_z(d)))
        if PRE:
            for d in FAR:
                second.append(copies.start(a.at[cz * 4], a.at[cz * 4], at_z(d)))
                second.append(copies.start(b.at[cx * 4], b.at[cx * 4], at_x(d)))
        skip = 1 if PRE else 0

        def middle():
            arrived(first_a + first_b)
            batch = []
            for ref, base, at in ((a, cz * 4, at_z), (b, cx * 4, at_x)):
                rows = pl.ds(base + skip, 4 - skip)
                for d in FAR:
                    batch.append(copies.start(ref.at[rows], ref.at[rows], at(d)))
            return second + batch

        return middle

    def alias_spread(i, h):
        halves = (
            (sa[i][h], ra[i][h], ta[i][h], qa[i][h], cx, cz, at_x, at_z),
            (sb[i][h], rb[i][h], tb[i][h], qb[i][h], cz, cx, at_z, at_x),
        )
        firsts = [[], []]
        for low, high in CHUNKS:
            for k, (sx, rx, tx, qx, near, far, at_near, at_far) in enumerate(halves):
                for m in range(4):
                    for pos in range(low, high):
                        other = lax.rem(near + 3 - pos, 4)
                        block = other * 4 + m if k == 0 else m * 4 + other
                        part = run[plan[A_LAST, block] + 1, h * R : (h + 1) * R, k * B : (k + 1) * B]
                        sx[m, pos] = part.astype(BF16)
                span = pl.ds(low, high - low)
                firsts[k].append(
                    [
                        copies.start(sx.at[lax.rem(far + d, 4), span], rx.at[n, span], at_far(d))
                        for n, d in enumerate(FAR)
                    ]
                )

        def middle():
            second = []
            for c, (low, high) in enumerate(CHUNKS):
                for k, (sx, rx, tx, qx, near, far, at_near, at_far) in enumerate(halves):
                    arrived(firsts[k][c])
                    for pos in range(low, min(high, 3)):
                        total = sx[far, pos].astype(F32)
                        for n in range(3):
                            total = total + rx[n, pos].astype(F32)
                        tx[pos] = total
                        second.append(copies.start(tx.at[pos], qx.at[pos], at_near(3 - pos)))
            return second

        def end(second):
            arrived(second)
            sums = []
            for sx, rx, tx, qx, near, far, at_near, at_far in halves:
                total = sx[far, 3].astype(F32)
                for n in range(3):
                    total = total + rx[n, 3].astype(F32)
                for n in range(3):
                    total = total + qx[n]
                sums.append(total)
            return jnp.concatenate(sums, axis=1)

        return middle, end

    def entity_gather(ref, values):
        own = pl.ds(row * 2, 2)
        for n in range(2):
            ref[row * 2 + n] = values[n]
        first = []
        first.extend([copies.start(ref.at[own], ref.at[own], at_y(d)) for d in FAR])
        second = [copies.start(ref.at[own], ref.at[own], mate)]

        def middle():
            for cp, d in zip(first, FAR):
                cp.wait_recv()
                came = pl.ds((lax.rem(cy + 4 - d, 4) * 2 + cc) * 2, 2)
                second.append(copies.start(ref.at[came], ref.at[came], mate))
            return second

        return middle

    def entity_spread(i, h):
        sx, mx, tx, qx = se[i][h], me[i][h], te[i][h], qe[i][h]
        first = []
        for n, d in enumerate(FAR + (0,)):
            y = lax.rem(cy + d, 4)
            for c in range(2):
                for m in range(2):
                    sx[c, n, m] = run[plan[E_LAST, (y * 2 + c) * 2 + m] + 1, h * R : (h + 1) * R]
            first.append(copies.start(sx.at[1 - cc, n], mx.at[n], mate))

        def middle():
            second = []
            for n, d in enumerate(FAR):
                first[n].wait_recv()
                for m in range(2):
                    tx[n, m] = (sx[cc, n, m] + mx[n, m]).astype(BF16)
                second.append(copies.start(tx.at[n], qx.at[n], at_y(d)))
            first[3].wait_recv()
            return second

        def end(second):
            arrived(second)
            parts = []
            for m in range(2):
                total = sx[cc, 3, m] + mx[3, m]
                for n in range(3):
                    total = total + qx[n, m].astype(F32)
                parts.append(total)
            return parts

        return middle, end

    nt = (((1,), (1,)), ((), ()))
    nn = (((1,), (0,)), ((), ()))

    def tiles(load_row, load_pair, wx, sx, rows, mode):
        tile_row, keep_row = rows

        def body(q, carry):
            products, pairs, errors = [], [], []
            for u in range(STEP):
                p = q * STEP + u
                mine = load_row(2 * p)
                pair = load_pair(p)
                products.append(lax.dot_general(mine, pair, nt, preferred_element_type=F32))
                pairs.append(pair)
            for u in range(STEP):
                p = q * STEP + u
                t0, t1 = plan[tile_row, 2 * p], plan[tile_row, 2 * p + 1]
                weight = jnp.concatenate([wx[t0], wx[t1]], axis=1).astype(F32)
                if mode == "resid":
                    score = jnp.concatenate([sx[t0], sx[t1]], axis=1).astype(F32)
                    errors.append((weight * (score - products[u])).astype(BF16))
                elif mode == "image":
                    errors.append((weight * products[u]).astype(BF16))
                else:
                    errors.append(weight * products[u] * products[u])
            for u in range(STEP):
                p = q * STEP + u
                keep = plan[keep_row, 2 * p].astype(F32)
                if mode == "curve":
                    term = errors[u][:, :B] + errors[u][:, B:]
                    run_c[p + 1] = run_c[p] * keep + term
                else:
                    term = lax.dot_general(errors[u], pairs[u], nn, preferred_element_type=F32)
                    run[p + 1] = run[p] * keep + term
            return carry

        lax.fori_loop(0, PAIRS // STEP, body, 0)

    def alias_tiles(i, mode):
        def load_row(n):
            left = jnp.concatenate([ga[i][h][plan[A_SWAP, n]] for h in range(NS)], axis=0)
            right = jnp.concatenate([gb[i][h][plan[A_KEY, n]] for h in range(NS)], axis=0)
            return jnp.concatenate([left, right], axis=1)

        def load_pair(p):
            e0, e1 = plan[A_OTHER, 2 * p], plan[A_OTHER, 2 * p + 1]
            return jnp.concatenate([gy0[e0], gy0[e1]], axis=0)

        tiles(load_row, load_pair, w, s, (A_TILE, A_KEEP), mode)

    def entity_tiles(i, mode):
        def load_row(n):
            if i == 0:
                return gy0[plan[E_KEY, n]]
            return jnp.concatenate([gy[i - 1][h][plan[E_KEY, n]] for h in range(NS)], axis=0)

        def load_pair(p):
            a0, a1 = plan[E_OTHER, 2 * p], plan[E_OTHER, 2 * p + 1]
            return jnp.concatenate([xn[a0], xn[a1]], axis=0)

        tiles(load_row, load_pair, wt, st, (E_TILE, E_KEEP), mode)

    def flip(source, target, low, high):
        def body(n, carry):
            for u in range(4):
                target[low + 4 * n + u] = source[low + 4 * n + u].T
            return carry

        lax.fori_loop(0, (high - low) // 4, body, 0)

    def curve_row(last):
        block = run_c[last + 1]
        high = block.astype(BF16)
        low = (block - high.astype(F32)).astype(BF16)
        ones = jnp.ones((16, B), BF16)
        total = lax.dot_general(ones, high, nt, preferred_element_type=F32)
        total = total + lax.dot_general(ones, low, nt, preferred_element_type=F32)
        return total[0:1]

    def first_step(x, r, image_of):
        d = r
        rr = jnp.sum(r * r, axis=-1, keepdims=True)
        image = image_of + ridge * d
        step = rr / (jnp.sum(d * image, axis=-1, keepdims=True) + eps)
        x = x + step * d
        r = r - step * image
        new = jnp.sum(r * r, axis=-1, keepdims=True)
        d = r + (new / (rr + eps)) * d
        return x, d, new

    flips = [
        (src, dst, n, n + 16) for src, dst in ((w, wt), (s, st)) for n in range(0, T, 16)
    ]

    def together(streams):
        streams = list(streams)
        while streams:
            for stream in list(streams):
                try:
                    next(stream)
                except StopIteration:
                    streams.remove(stream)

    def gap():
        for n in range(3):
            if flips:
                flip(*flips.pop(0))

    y_gather = []

    def alias_stream(h):
        rows = pl.ds(h * R, R)
        x0 = x_in[rows, :]
        mid = alias_gather(0, h, x0)
        if h == 0:
            own_y = [y_in[pl.ds(0, B), :], y_in[pl.ds(B, B), :]]
            y_gather.append(entity_gather(gy0, own_y))
            load_w.start()
            load_s.start()
        yield
        second = mid()
        if h == NS - 1:
            tile_plan(ids, plan_v, cx, cz)
            load_plan.start()
            run[0] = jnp.zeros((B, K), F32)
            run_c[0] = jnp.zeros((B, B), F32)
            emsg[...] = jnp.zeros_like(emsg)
            load_plan.wait()
            load_w.wait()
            load_s.wait()
            zero = jnp.zeros((B, B), BF16)
            for ref in (w, s, wt, st):
                ref[T] = zero
            y_gather.append(y_gather[0]())
            gap()
        yield
        arrived(second)
        if h == NS - 1:
            arrived(y_gather[1])
            alias_tiles(0, "resid")
        yield
        middle, end = alias_spread(0, h)
        if h == NS - 1:
            gap()
        yield
        second = middle()
        yield
        image = end(second)
        x = x_in[rows, :].astype(F32)
        r = image - ridge * x
        vr[rows, :] = r
        mid = alias_gather(1, h, r.astype(BF16))
        yield
        second = mid()
        if h == NS - 1:
            gap()
        yield
        arrived(second)
        if h == NS - 1:
            alias_tiles(1, "image")
        yield
        middle, end = alias_spread(1, h)
        if h == NS - 1:
            gap()
        yield
        second = middle()
        yield
        image = end(second)
        x1, d1, rr1 = first_step(x_in[rows, :].astype(F32), vr[rows, :], image)
        mid = alias_gather(2, h, d1.astype(BF16))
        vd[rows, :] = d1
        vx[rows, :] = x1
        vn[rows, :] = jnp.broadcast_to(rr1, (R, B))
        vq[rows, :] = jnp.broadcast_to(ridge * jnp.sum(d1 * d1, axis=-1, keepdims=True), (R, B))
        yield
        second = mid()
        if h == NS - 1:
            gap()
        yield
        mid_x = alias_gather(3, h, vx[rows, :].astype(BF16))
        arrived(second)
        yield
        x_gather.extend(mid_x())
        if h == NS - 1:
            alias_tiles(2, "curve")

    x_gather = []
    together([alias_stream(h) for h in range(NS)])
    while flips:
        flip(*flips.pop(0))
    own_dd = jnp.sum(vq[...] * eye, axis=0, keepdims=True)
    own_rr = jnp.sum(vn[...] * eye, axis=0, keepdims=True)
    for b in range(NB):
        line = curve_row(plan[A_LAST, b])
        cmsg[0, pl.ds(b, 1), :] = line + jnp.where(col == b, own_dd, 0.0)
        cmsg[0, pl.ds(NB + b, 1), :] = jnp.where(col == b, own_rr, 0.0)
    arrived([copies.start(cmsg.at[0], cmsg.at[4 - d], at_x(d)) for d in FAR])
    csum[0] = (cmsg[0] + cmsg[1]) + (cmsg[2] + cmsg[3])
    small = [copies.start(csum.at[0], csum.at[4 - d], at_z(d)) for d in FAR]
    arrived(x_gather)
    arrived(small)
    total = (csum[0] + csum[1]) + (csum[2] + csum[3])
    rates = total[NB:] / (total[:NB] + eps)
    for b in range(NB):
        step = to_column(rates[b : b + 1])
        a_slot = (b % 4) * 4 + lax.rem(b // 4 + 4 - cx, 4)
        b_slot = (b // 4) * 4 + lax.rem(b % 4 + 4 - cz, 4)
        for h in range(NS):
            cut = slice(h * R, (h + 1) * R)
            left = ga[3][h][a_slot].astype(F32) + step[cut] * ga[2][h][a_slot].astype(F32)
            right = gb[3][h][b_slot].astype(F32) + step[cut] * gb[2][h][b_slot].astype(F32)
            xn[b, cut] = jnp.concatenate([left, right], axis=1).astype(BF16)

    def entity_stream(h):
        halves = [pl.ds(m * B + h * R, R) for m in range(2)]
        if h == 0:
            entity_tiles(0, "resid")
        middle, end = entity_spread(0, h)
        yield
        second = middle()
        yield
        parts = end(second)
        rs = [parts[m] - ridge * y_in[halves[m], :].astype(F32) for m in range(2)]
        mid = entity_gather(gy[0][h], [r.astype(BF16) for r in rs])
        for m in range(2):
            ur[halves[m], :] = rs[m]
        yield
        second = mid()
        yield
        arrived(second)
        if h == NS - 1:
            entity_tiles(1, "image")
        yield
        middle, end = entity_spread(1, h)
        yield
        second = middle()
        yield
        parts = end(second)
        steps = [
            first_step(y_in[halves[m], :].astype(F32), ur[halves[m], :], parts[m])
            for m in range(2)
        ]
        mid = entity_gather(gy[1][h], [step[1].astype(BF16) for step in steps])
        for m, (y1, d1, rr1) in enumerate(steps):
            ux[halves[m], :] = y1
            ud[halves[m], :] = d1
            un[halves[m], :] = jnp.broadcast_to(rr1, (R, B))
            uq[halves[m], :] = jnp.broadcast_to(
                ridge * jnp.sum(d1 * d1, axis=-1, keepdims=True), (R, B)
            )
        yield
        second = mid()
        yield
        arrived(second)
        if h == NS - 1:
            entity_tiles(2, "curve")

    together([entity_stream(h) for h in range(NS)])
    for n, d in enumerate(FAR + (0,)):
        y = lax.rem(cy + d, 4)
        for c in range(2):
            for m in range(2):
                emsg[c, n, m : m + 1] = curve_row(plan[E_LAST, (y * 2 + c) * 2 + m])
    first = copies.start(emsg.at[1 - cc], ecome, mate)
    mine = jnp.sum(
        jnp.where(lax.broadcasted_iota(jnp.int32, (NB, B), 0) == col, rates, 0.0),
        axis=0, keepdims=True,
    )
    x_out[...] = (vx[...] + to_column(mine) * vd[...]).astype(BF16)
    arrived([first])
    small = []
    for n, d in enumerate(FAR):
        esum[n] = emsg[cc, n] + ecome[n]
        small.append(copies.start(esum.at[n], elast.at[n], at_y(d)))
    total = emsg[cc, 3] + ecome[3]
    copies.flush(copies.all[:-3])
    arrived(small)
    for n in range(3):
        total = total + elast[n]
    for m in range(2):
        rows = pl.ds(m * B, B)
        step = un[rows, :][:, :1] / (to_column(total[m : m + 1]) + uq[rows, :][:, :1] + eps)
        y_out[rows, :] = (ux[rows, :] + step * ud[rows, :]).astype(BF16)
    copies.flush(copies.all)


def emit_kernel(x_in, y_in, x_out, y_out):
    x_out[...] = x_in[...]
    y_out[...] = y_in[...]


def on_device(alias_factors, entity_factors, tile_ids, tile_score, tile_weight):
    vmem = pl.BlockSpec(memory_space=pltpu.VMEM)
    hbm = pl.BlockSpec(memory_space=pl.ANY)
    V = pltpu.VMEM

    def each(n, shape, dtype):
        return [[V(shape, dtype) for h in range(NS)] for i in range(n)]

    results = pl.pallas_call(
        sweep_kernel,
        name="als_sweep",
        out_shape=(
            jax.ShapeDtypeStruct((B, K), BF16),
            jax.ShapeDtypeStruct((2 * B, K), BF16),
        ),
        in_specs=[vmem, hbm, hbm, hbm, hbm],
        out_specs=(vmem, vmem),
        scratch_shapes=[
            V((T + 1, B, B), BF16), V((T + 1, B, B), BF16),
            V((T + 1, B, B), BF16), V((T + 1, B, B), BF16),
            V((NB, B, K), BF16),
            V((PAIRS + 1, B, K), F32), V((PAIRS + 1, B, B), F32),
            each(4, (NB, R, B), BF16), each(4, (NB, R, B), BF16),
            V((NB, B, K), BF16), each(2, (NB, R, K), BF16),
            each(2, (4, 4, R, B), BF16), each(2, (4, 4, R, B), BF16),
            each(2, (3, 4, R, B), BF16), each(2, (3, 4, R, B), BF16),
            each(2, (3, R, B), F32), each(2, (3, R, B), F32),
            each(2, (3, R, B), F32), each(2, (3, R, B), F32),
            each(2, (2, 4, 2, R, K), F32), each(2, (4, 2, R, K), F32),
            each(2, (3, 2, R, K), BF16), each(2, (3, 2, R, K), BF16),
            V((4, 2 * NB, B), F32), V((4, 2 * NB, B), F32),
            V((2, 4, 8, B), F32), V((4, 8, B), F32), V((3, 8, B), F32), V((3, 8, B), F32),
            V((B, K), F32), V((B, K), F32), V((B, K), F32), V((B, B), F32), V((B, B), F32),
            V((2 * B, K), F32), V((2 * B, K), F32), V((2 * B, K), F32),
            V((2 * B, B), F32), V((2 * B, B), F32),
            V((B, K), BF16), V((2 * B, K), BF16),
            V((16, 128), jnp.int32), pltpu.SMEM((16, 128), jnp.int32),
            pltpu.SemaphoreType.DMA((N_COPIES,)),
            pltpu.SemaphoreType.DMA((N_COPIES,)),
            pltpu.SemaphoreType.DMA((5,)),
        ],
        compiler_params=pltpu.CompilerParams(
            collective_id=0, has_side_effects=True, vmem_limit_bytes=60 * 2**20
        ),
    )(tile_ids[0, 0].T, alias_factors, entity_factors, tile_weight, tile_score)
    return pl.pallas_call(
        emit_kernel,
        name="emit",
        out_shape=(
            jax.ShapeDtypeStruct((B, K), BF16),
            jax.ShapeDtypeStruct((2 * B, K), BF16),
        ),
    )(*results)


def solution(mesh):
    placed = (
        P(("row", "col"), None),
        P(("row", "col"), None),
        P("row", "col", None, None),
        P("row", "col", None, None, None),
        P("row", "col", None, None, None),
    )
    return jax.shard_map(
        on_device,
        mesh=mesh,
        in_specs=placed,
        out_specs=(P(("row", "col"), None), P(("row", "col"), None)),
        check_vma=False,
    )
```

```python
import functools

import jax
import jax.numpy as jnp
from jax import lax
from jax.experimental import pallas as pl
from jax.experimental.pallas import tpu as pltpu
from jax.sharding import PartitionSpec as P

ridge = 1.0
eps = 1e-06
MESH = pl.DeviceIdType.MESH
F32 = jnp.float32
BF16 = jnp.bfloat16
B = 128
K = 256
T = 96
NB = 16
PAIRS = (T + NB) // 2
STEP = 28
NS = 2
R = B // NS
CHUNKS = ((0, 4),)
PRE = True

A_TILE, A_OTHER, A_KEY, A_SWAP, A_KEEP, A_LAST = range(6)
E_TILE, E_OTHER, E_KEY, E_KEEP, E_LAST = range(6, 11)
TOPS = (T, 15, 15, 15, 1, PAIRS - 1, T, 15, 15, 1, PAIRS - 1)


def tile_plan(ids_ref, out_ref, cx, cz):
    ids = ids_ref[...].astype(F32)
    row_i = lax.broadcasted_iota(jnp.int32, (T, 128), 0).astype(F32)
    lane_i = lax.broadcasted_iota(jnp.int32, (T, 128), 1).astype(F32)
    row_t = lax.broadcasted_iota(jnp.int32, (T, T), 0).astype(F32)
    lane_t = lax.broadcasted_iota(jnp.int32, (T, T), 1).astype(F32)
    cx, cz = cx.astype(F32), cz.astype(F32)
    out_ref[...] = jnp.zeros_like(out_ref)

    def put(row, value):
        top = TOPS[row]
        out_ref[row : row + 1, :] = jnp.minimum(jnp.maximum(value.astype(jnp.int32), 0), top)

    lines = [jnp.broadcast_to(ids[n : n + 1, :], (T, T)) for n in range(2)]
    columns = [
        jnp.sum(jnp.where(row_t == lane_t, line, 0.0), axis=1, keepdims=True) for line in lines
    ]
    for key, rows in (
        (0, (A_TILE, A_OTHER, A_KEY, A_KEEP, A_LAST)),
        (1, (E_TILE, E_OTHER, E_KEY, E_KEEP, E_LAST)),
    ):
        kc = jnp.broadcast_to(columns[key], (T, 128))
        oc = jnp.broadcast_to(columns[1 - key], (T, 128))
        same = jnp.where(jnp.broadcast_to(columns[key], (T, T)) == lines[key], 1.0, 0.0)
        rank = jnp.sum(jnp.where(lane_t < row_t, same, 0.0), axis=1, keepdims=True)
        count = jnp.sum(same, axis=1, keepdims=True)
        odd = count - 2.0 * jnp.floor(count * 0.5)
        width = jnp.broadcast_to(1.0 + jnp.where(rank == 0.0, odd, 0.0), (T, 128))
        n_row = jnp.sum(jnp.where(kc == lane_i, width, 0.0), axis=0, keepdims=True)
        start = jnp.sum(
            jnp.where(lane_i < kc, jnp.broadcast_to(n_row, (T, 128)), 0.0), axis=1, keepdims=True
        )
        pos = jnp.broadcast_to(start + rank, (T, 128))
        hit = jnp.where(pos == lane_i, 1.0, 0.0)
        valid = jnp.sum(hit, axis=0, keepdims=True)
        put(rows[0], jnp.sum(hit * row_i, axis=0, keepdims=True) + T * (1.0 - valid))
        put(rows[1], jnp.sum(hit * oc, axis=0, keepdims=True))
        key_row = jnp.sum(hit * kc, axis=0, keepdims=True)
        if key == 0:
            high = jnp.floor(key_row * 0.25)
            low = key_row - 4.0 * high
            put(A_KEY, high * 4.0 + low - cz + jnp.where(low < cz, 4.0, 0.0))
            put(A_SWAP, low * 4.0 + high - cx + jnp.where(high < cx, 4.0, 0.0))
        else:
            put(rows[2], key_row)
        keep = jnp.where(jnp.broadcast_to(rank, (T, 128)) > 0.0, hit, 0.0)
        put(rows[3], jnp.sum(keep, axis=0, keepdims=True))
        upto = jnp.sum(jnp.where(kc <= lane_i, width, 0.0), axis=0, keepdims=True)
        put(rows[4], upto * 0.5 - 1.0)


class Copies:
    def __init__(self, send, recv):
        self.send, self.recv, self.all, self.done, self.batch = send, recv, [], [], []

    def start(self, src, dst, device):
        n = len(self.all)
        cp = pltpu.make_async_remote_copy(
            src_ref=src,
            dst_ref=dst,
            send_sem=self.send.at[n],
            recv_sem=self.recv.at[n],
            device_id=device,
            device_id_type=MESH,
        )
        cp.start()
        self.all.append(cp)
        return cp

    def flush(self, some):
        for cp in some:
            if not any(cp is other for other in self.done):
                cp.wait_send()
                self.done.append(cp)


N_GATHER = 18 if PRE else 12
N_COPIES = NS * (N_GATHER * 4 + (6 * len(CHUNKS) + 6) * 2 + 7 * 2 + 7 * 2) + 7 + 6 + 4
FAR = (1, 3, 2)


def sweep_kernel(
    ids, x_hbm, y_hbm, w_hbm, s_hbm, x_out, y_out,
    w, s, wt, st, xn, run, run_c, ga, gb, gy0, gy, sa, sb, ra, rb, ta, tb, qa, qb,
    se, me, te, qe, cmsg, csum, emsg, ecome, esum, elast, vx, vr, vd, vn, vq, ux, ur, ud, un, uq,
    x_in, y_in, plan_v, plan, send, recv, lsem,
):
    row = lax.axis_index("row")
    col = lax.axis_index("col")
    cy, cc = row // 2, row % 2
    cx, cz = col // 4, col % 4

    def at_x(d):
        return (row, lax.rem(cx + d, 4) * 4 + cz)

    def at_z(d):
        return (row, cx * 4 + lax.rem(cz + d, 4))

    def at_y(d):
        return (lax.rem(cy + d, 4) * 2 + cc, col)

    mate = (cy * 2 + (1 - cc), col)

    copies = Copies(send, recv)
    load_w = pltpu.make_async_copy(w_hbm.at[0, 0], w.at[pl.ds(0, T)], lsem.at[0])
    load_s = pltpu.make_async_copy(s_hbm.at[0, 0], s.at[pl.ds(0, T)], lsem.at[1])
    load_plan = pltpu.make_async_copy(plan_v, plan, lsem.at[2])
    load_x = pltpu.make_async_copy(x_hbm, x_in, lsem.at[3])
    load_y = pltpu.make_async_copy(y_hbm, y_in, lsem.at[4])
    load_x.start()
    load_y.start()

    barrier = pltpu.get_barrier_semaphore()
    for peer in [at(d) for at in (at_x, at_z, at_y) for d in FAR] + [mate]:
        pl.semaphore_signal(barrier, 1, device_id=peer, device_id_type=MESH)
    pl.semaphore_wait(barrier, 10)

    eye = jnp.where(
        lax.broadcasted_iota(jnp.int32, (B, B), 0) == lax.broadcasted_iota(jnp.int32, (B, B), 1),
        1.0, 0.0,
    ).astype(F32)

    def to_row(column):
        return jnp.sum(jnp.broadcast_to(column, (B, B)) * eye, axis=0, keepdims=True)

    def to_column(line):
        return jnp.sum(jnp.broadcast_to(line, (B, B)) * eye, axis=1, keepdims=True)

    def arrived(list_of_copies):
        for cp in list_of_copies:
            cp.wait_recv()

    load_x.wait()
    load_y.wait()

    def alias_gather(i, h, value):
        a, b = ga[i][h], gb[i][h]
        a[cz * 4] = value[:, :B]
        b[cx * 4] = value[:, B:]
        first_a, first_b, second = [], [], []
        for d in FAR:
            first_a.append(copies.start(a.at[cz * 4], a.at[cz * 4 + 4 - d], at_x(d)))
            first_b.append(copies.start(b.at[cx * 4], b.at[cx * 4 + 4 - d], at_z(d)))
        if PRE:
            for d in FAR:
                second.append(copies.start(a.at[cz * 4], a.at[cz * 4], at_z(d)))
                second.append(copies.start(b.at[cx * 4], b.at[cx * 4], at_x(d)))
        skip = 1 if PRE else 0

        def middle():
            arrived(first_a + first_b)
            batch = []
            for ref, base, at in ((a, cz * 4, at_z), (b, cx * 4, at_x)):
                rows = pl.ds(base + skip, 4 - skip)
                for d in FAR:
                    batch.append(copies.start(ref.at[rows], ref.at[rows], at(d)))
            return second + batch

        return middle

    def alias_spread(i, h):
        halves = (
            (sa[i][h], ra[i][h], ta[i][h], qa[i][h], cx, cz, at_x, at_z),
            (sb[i][h], rb[i][h], tb[i][h], qb[i][h], cz, cx, at_z, at_x),
        )
        firsts = [[], []]
        for low, high in CHUNKS:
            for k, (sx, rx, tx, qx, near, far, at_near, at_far) in enumerate(halves):
                for m in range(4):
                    for pos in range(low, high):
                        other = lax.rem(near + 3 - pos, 4)
                        block = other * 4 + m if k == 0 else m * 4 + other
                        part = run[plan[A_LAST, block] + 1, h * R : (h + 1) * R, k * B : (k + 1) * B]
                        sx[m, pos] = part.astype(BF16)
                span = pl.ds(low, high - low)
                firsts[k].append(
                    [
                        copies.start(sx.at[lax.rem(far + d, 4), span], rx.at[n, span], at_far(d))
                        for n, d in enumerate(FAR)
                    ]
                )

        def middle():
            second = []
            for c, (low, high) in enumerate(CHUNKS):
                for k, (sx, rx, tx, qx, near, far, at_near, at_far) in enumerate(halves):
                    arrived(firsts[k][c])
                    for pos in range(low, min(high, 3)):
                        total = sx[far, pos].astype(F32)
                        for n in range(3):
                            total = total + rx[n, pos].astype(F32)
                        tx[pos] = total
                        second.append(copies.start(tx.at[pos], qx.at[pos], at_near(3 - pos)))
            return second

        def end(second):
            arrived(second)
            sums = []
            for sx, rx, tx, qx, near, far, at_near, at_far in halves:
                total = sx[far, 3].astype(F32)
                for n in range(3):
                    total = total + rx[n, 3].astype(F32)
                for n in range(3):
                    total = total + qx[n]
                sums.append(total)
            return jnp.concatenate(sums, axis=1)

        return middle, end

    def entity_gather(ref, values):
        own = pl.ds(row * 2, 2)
        for n in range(2):
            ref[row * 2 + n] = values[n]
        first = []
        first.extend([copies.start(ref.at[own], ref.at[own], at_y(d)) for d in FAR])
        second = [copies.start(ref.at[own], ref.at[own], mate)]

        def middle():
            for cp, d in zip(first, FAR):
                cp.wait_recv()
                came = pl.ds((lax.rem(cy + 4 - d, 4) * 2 + cc) * 2, 2)
                second.append(copies.start(ref.at[came], ref.at[came], mate))
            return second

        return middle

    def entity_spread(i, h):
        sx, mx, tx, qx = se[i][h], me[i][h], te[i][h], qe[i][h]
        first = []
        for n, d in enumerate(FAR + (0,)):
            y = lax.rem(cy + d, 4)
            for c in range(2):
                for m in range(2):
                    sx[c, n, m] = run[plan[E_LAST, (y * 2 + c) * 2 + m] + 1, h * R : (h + 1) * R]
            first.append(copies.start(sx.at[1 - cc, n], mx.at[n], mate))

        def middle():
            second = []
            for n, d in enumerate(FAR):
                first[n].wait_recv()
                for m in range(2):
                    tx[n, m] = (sx[cc, n, m] + mx[n, m]).astype(BF16)
                second.append(copies.start(tx.at[n], qx.at[n], at_y(d)))
            first[3].wait_recv()
            return second

        def end(second):
            arrived(second)
            parts = []
            for m in range(2):
                total = sx[cc, 3, m] + mx[3, m]
                for n in range(3):
                    total = total + qx[n, m].astype(F32)
                parts.append(total)
            return parts

        return middle, end

    nt = (((1,), (1,)), ((), ()))
    nn = (((1,), (0,)), ((), ()))

    def tiles(load_row, load_pair, wx, sx, rows, mode):
        tile_row, keep_row = rows

        def body(q, carry):
            products, pairs, errors = [], [], []
            for u in range(STEP):
                p = q * STEP + u
                mine = load_row(2 * p)
                pair = load_pair(p)
                products.append(lax.dot_general(mine, pair, nt, preferred_element_type=F32))
                pairs.append(pair)
            for u in range(STEP):
                p = q * STEP + u
                t0, t1 = plan[tile_row, 2 * p], plan[tile_row, 2 * p + 1]
                weight = jnp.concatenate([wx[t0], wx[t1]], axis=1).astype(F32)
                if mode == "resid":
                    score = jnp.concatenate([sx[t0], sx[t1]], axis=1).astype(F32)
                    errors.append((weight * (score - products[u])).astype(BF16))
                elif mode == "image":
                    errors.append((weight * products[u]).astype(BF16))
                else:
                    errors.append(weight * products[u] * products[u])
            for u in range(STEP):
                p = q * STEP + u
                keep = plan[keep_row, 2 * p].astype(F32)
                if mode == "curve":
                    term = errors[u][:, :B] + errors[u][:, B:]
                    run_c[p + 1] = run_c[p] * keep + term
                else:
                    term = lax.dot_general(errors[u], pairs[u], nn, preferred_element_type=F32)
                    run[p + 1] = run[p] * keep + term
            return carry

        lax.fori_loop(0, PAIRS // STEP, body, 0)

    def alias_tiles(i, mode):
        def load_row(n):
            left = jnp.concatenate([ga[i][h][plan[A_SWAP, n]] for h in range(NS)], axis=0)
            right = jnp.concatenate([gb[i][h][plan[A_KEY, n]] for h in range(NS)], axis=0)
            return jnp.concatenate([left, right], axis=1)

        def load_pair(p):
            e0, e1 = plan[A_OTHER, 2 * p], plan[A_OTHER, 2 * p + 1]
            return jnp.concatenate([gy0[e0], gy0[e1]], axis=0)

        tiles(load_row, load_pair, w, s, (A_TILE, A_KEEP), mode)

    def entity_tiles(i, mode):
        def load_row(n):
            if i == 0:
                return gy0[plan[E_KEY, n]]
            return jnp.concatenate([gy[i - 1][h][plan[E_KEY, n]] for h in range(NS)], axis=0)

        def load_pair(p):
            a0, a1 = plan[E_OTHER, 2 * p], plan[E_OTHER, 2 * p + 1]
            return jnp.concatenate([xn[a0], xn[a1]], axis=0)

        tiles(load_row, load_pair, wt, st, (E_TILE, E_KEEP), mode)

    def flip(source, target, low, high):
        def body(n, carry):
            for u in range(4):
                target[low + 4 * n + u] = source[low + 4 * n + u].T
            return carry

        lax.fori_loop(0, (high - low) // 4, body, 0)

    def curve_row(last):
        block = run_c[last + 1]
        high = block.astype(BF16)
        low = (block - high.astype(F32)).astype(BF16)
        ones = jnp.ones((16, B), BF16)
        total = lax.dot_general(ones, high, nt, preferred_element_type=F32)
        total = total + lax.dot_general(ones, low, nt, preferred_element_type=F32)
        return total[0:1]

    def first_step(x, r, image_of):
        d = r
        rr = jnp.sum(r * r, axis=-1, keepdims=True)
        image = image_of + ridge * d
        step = rr / (jnp.sum(d * image, axis=-1, keepdims=True) + eps)
        x = x + step * d
        r = r - step * image
        new = jnp.sum(r * r, axis=-1, keepdims=True)
        d = r + (new / (rr + eps)) * d
        return x, d, new

    flips = [
        (src, dst, n, n + 16) for src, dst in ((w, wt), (s, st)) for n in range(0, T, 16)
    ]

    def together(streams):
        streams = list(streams)
        while streams:
            for stream in list(streams):
                try:
                    next(stream)
                except StopIteration:
                    streams.remove(stream)

    def gap():
        for n in range(3):
            if flips:
                flip(*flips.pop(0))

    y_gather = []

    def alias_stream(h):
        rows = pl.ds(h * R, R)
        x0 = x_in[rows, :]
        mid = alias_gather(0, h, x0)
        if h == 0:
            own_y = [y_in[pl.ds(0, B), :], y_in[pl.ds(B, B), :]]
            y_gather.append(entity_gather(gy0, own_y))
            load_w.start()
            load_s.start()
        yield
        second = mid()
        if h == NS - 1:
            tile_plan(ids, plan_v, cx, cz)
            load_plan.start()
            run[0] = jnp.zeros((B, K), F32)
            run_c[0] = jnp.zeros((B, B), F32)
            emsg[...] = jnp.zeros_like(emsg)
            load_plan.wait()
            load_w.wait()
            load_s.wait()
            zero = jnp.zeros((B, B), BF16)
            for ref in (w, s, wt, st):
                ref[T] = zero
            y_gather.append(y_gather[0]())
            gap()
        yield
        arrived(second)
        if h == NS - 1:
            arrived(y_gather[1])
            alias_tiles(0, "resid")
        yield
        middle, end = alias_spread(0, h)
        if h == NS - 1:
            gap()
        yield
        second = middle()
        yield
        image = end(second)
        x = x_in[rows, :].astype(F32)
        r = image - ridge * x
        vr[rows, :] = r
        mid = alias_gather(1, h, r.astype(BF16))
        yield
        second = mid()
        if h == NS - 1:
            gap()
        yield
        arrived(second)
        if h == NS - 1:
            alias_tiles(1, "image")
        yield
        middle, end = alias_spread(1, h)
        if h == NS - 1:
            gap()
        yield
        second = middle()
        yield
        image = end(second)
        x1, d1, rr1 = first_step(x_in[rows, :].astype(F32), vr[rows, :], image)
        mid = alias_gather(2, h, d1.astype(BF16))
        vd[rows, :] = d1
        vx[rows, :] = x1
        vn[rows, :] = jnp.broadcast_to(rr1, (R, B))
        vq[rows, :] = jnp.broadcast_to(ridge * jnp.sum(d1 * d1, axis=-1, keepdims=True), (R, B))
        yield
        second = mid()
        mid_x = alias_gather(3, h, vx[rows, :].astype(BF16))
        if h == NS - 1:
            gap()
        yield
        x_gather.extend(mid_x())
        arrived(second)
        if h == NS - 1:
            alias_tiles(2, "curve")

    x_gather = []
    together([alias_stream(h) for h in range(NS)])
    while flips:
        flip(*flips.pop(0))
    own_dd = jnp.sum(vq[...] * eye, axis=0, keepdims=True)
    own_rr = jnp.sum(vn[...] * eye, axis=0, keepdims=True)
    for b in range(NB):
        line = curve_row(plan[A_LAST, b])
        cmsg[0, pl.ds(b, 1), :] = line + jnp.where(col == b, own_dd, 0.0)
        cmsg[0, pl.ds(NB + b, 1), :] = jnp.where(col == b, own_rr, 0.0)
    arrived([copies.start(cmsg.at[0], cmsg.at[4 - d], at_x(d)) for d in FAR])
    csum[0] = (cmsg[0] + cmsg[1]) + (cmsg[2] + cmsg[3])
    small = [copies.start(csum.at[0], csum.at[4 - d], at_z(d)) for d in FAR]
    arrived(x_gather)
    arrived(small)
    total = (csum[0] + csum[1]) + (csum[2] + csum[3])
    rates = total[NB:] / (total[:NB] + eps)
    for b in range(NB):
        step = to_column(rates[b : b + 1])
        a_slot = (b % 4) * 4 + lax.rem(b // 4 + 4 - cx, 4)
        b_slot = (b // 4) * 4 + lax.rem(b % 4 + 4 - cz, 4)
        for h in range(NS):
            cut = slice(h * R, (h + 1) * R)
            left = ga[3][h][a_slot].astype(F32) + step[cut] * ga[2][h][a_slot].astype(F32)
            right = gb[3][h][b_slot].astype(F32) + step[cut] * gb[2][h][b_slot].astype(F32)
            xn[b, cut] = jnp.concatenate([left, right], axis=1).astype(BF16)

    def entity_stream(h):
        halves = [pl.ds(m * B + h * R, R) for m in range(2)]
        if h == 0:
            entity_tiles(0, "resid")
        middle, end = entity_spread(0, h)
        yield
        second = middle()
        yield
        parts = end(second)
        rs = [parts[m] - ridge * y_in[halves[m], :].astype(F32) for m in range(2)]
        mid = entity_gather(gy[0][h], [r.astype(BF16) for r in rs])
        for m in range(2):
            ur[halves[m], :] = rs[m]
        yield
        second = mid()
        yield
        arrived(second)
        if h == NS - 1:
            entity_tiles(1, "image")
        yield
        middle, end = entity_spread(1, h)
        yield
        second = middle()
        yield
        parts = end(second)
        steps = [
            first_step(y_in[halves[m], :].astype(F32), ur[halves[m], :], parts[m])
            for m in range(2)
        ]
        mid = entity_gather(gy[1][h], [step[1].astype(BF16) for step in steps])
        for m, (y1, d1, rr1) in enumerate(steps):
            ux[halves[m], :] = y1
            ud[halves[m], :] = d1
            un[halves[m], :] = jnp.broadcast_to(rr1, (R, B))
            uq[halves[m], :] = jnp.broadcast_to(
                ridge * jnp.sum(d1 * d1, axis=-1, keepdims=True), (R, B)
            )
        yield
        second = mid()
        yield
        arrived(second)
        if h == NS - 1:
            entity_tiles(2, "curve")

    together([entity_stream(h) for h in range(NS)])
    for n, d in enumerate(FAR + (0,)):
        y = lax.rem(cy + d, 4)
        for c in range(2):
            for m in range(2):
                emsg[c, n, m : m + 1] = curve_row(plan[E_LAST, (y * 2 + c) * 2 + m])
    first = copies.start(emsg.at[1 - cc], ecome, mate)
    mine = jnp.sum(
        jnp.where(lax.broadcasted_iota(jnp.int32, (NB, B), 0) == col, rates, 0.0),
        axis=0, keepdims=True,
    )
    x_out[...] = (vx[...] + to_column(mine) * vd[...]).astype(BF16)
    arrived([first])
    small = []
    for n, d in enumerate(FAR):
        esum[n] = emsg[cc, n] + ecome[n]
        small.append(copies.start(esum.at[n], elast.at[n], at_y(d)))
    total = emsg[cc, 3] + ecome[3]
    copies.flush(copies.all[:-3])
    arrived(small)
    for n in range(3):
        total = total + elast[n]
    for m in range(2):
        rows = pl.ds(m * B, B)
        step = un[rows, :][:, :1] / (to_column(total[m : m + 1]) + uq[rows, :][:, :1] + eps)
        y_out[rows, :] = (ux[rows, :] + step * ud[rows, :]).astype(BF16)
    copies.flush(copies.all)


def emit_kernel(x_in, y_in, x_out, y_out):
    x_out[...] = x_in[...]
    y_out[...] = y_in[...]


def on_device(alias_factors, entity_factors, tile_ids, tile_score, tile_weight):
    vmem = pl.BlockSpec(memory_space=pltpu.VMEM)
    hbm = pl.BlockSpec(memory_space=pl.ANY)
    V = pltpu.VMEM

    def each(n, shape, dtype):
        return [[V(shape, dtype) for h in range(NS)] for i in range(n)]

    results = pl.pallas_call(
        sweep_kernel,
        name="als_sweep",
        out_shape=(
            jax.ShapeDtypeStruct((B, K), BF16),
            jax.ShapeDtypeStruct((2 * B, K), BF16),
        ),
        in_specs=[vmem, hbm, hbm, hbm, hbm],
        out_specs=(vmem, vmem),
        scratch_shapes=[
            V((T + 1, B, B), BF16), V((T + 1, B, B), BF16),
            V((T + 1, B, B), BF16), V((T + 1, B, B), BF16),
            V((NB, B, K), BF16),
            V((PAIRS + 1, B, K), F32), V((PAIRS + 1, B, B), F32),
            each(4, (NB, R, B), BF16), each(4, (NB, R, B), BF16),
            V((NB, B, K), BF16), each(2, (NB, R, K), BF16),
            each(2, (4, 4, R, B), BF16), each(2, (4, 4, R, B), BF16),
            each(2, (3, 4, R, B), BF16), each(2, (3, 4, R, B), BF16),
            each(2, (3, R, B), F32), each(2, (3, R, B), F32),
            each(2, (3, R, B), F32), each(2, (3, R, B), F32),
            each(2, (2, 4, 2, R, K), F32), each(2, (4, 2, R, K), F32),
            each(2, (3, 2, R, K), BF16), each(2, (3, 2, R, K), BF16),
            V((4, 2 * NB, B), F32), V((4, 2 * NB, B), F32),
            V((2, 4, 8, B), F32), V((4, 8, B), F32), V((3, 8, B), F32), V((3, 8, B), F32),
            V((B, K), F32), V((B, K), F32), V((B, K), F32), V((B, B), F32), V((B, B), F32),
            V((2 * B, K), F32), V((2 * B, K), F32), V((2 * B, K), F32),
            V((2 * B, B), F32), V((2 * B, B), F32),
            V((B, K), BF16), V((2 * B, K), BF16),
            V((16, 128), jnp.int32), pltpu.SMEM((16, 128), jnp.int32),
            pltpu.SemaphoreType.DMA((N_COPIES,)),
            pltpu.SemaphoreType.DMA((N_COPIES,)),
            pltpu.SemaphoreType.DMA((5,)),
        ],
        compiler_params=pltpu.CompilerParams(
            collective_id=0, has_side_effects=True, vmem_limit_bytes=60 * 2**20
        ),
    )(tile_ids[0, 0].T, alias_factors, entity_factors, tile_weight, tile_score)
    return pl.pallas_call(
        emit_kernel,
        name="emit",
        out_shape=(
            jax.ShapeDtypeStruct((B, K), BF16),
            jax.ShapeDtypeStruct((2 * B, K), BF16),
        ),
    )(*results)


def solution(mesh):
    placed = (
        P(("row", "col"), None),
        P(("row", "col"), None),
        P("row", "col", None, None),
        P("row", "col", None, None, None),
        P("row", "col", None, None, None),
    )
    return jax.shard_map(
        on_device,
        mesh=mesh,
        in_specs=placed,
        out_specs=(P(("row", "col"), None), P(("row", "col"), None)),
        check_vma=False,
    )
```
